32 devices in a mesh: ctx: 8 (over z, y), tp: 4 (over x, core).
Axes of the slice: x: 2, y: 2, z: 4, core: 2. Of those that a mesh axis runs over, the one named last changes fastest.
Arguments:
- hidden: bfloat16 [2048, 2048], P('ctx', 'tp'), may hold values from -6 to 6
- norm_gain_a: float32 [2048], replicated, may hold values from 0.5 to 1.5
- in_weight_a: bfloat16 [3, 2048, 2048], P(None, 'ctx', 'tp'), may hold values from -0.125 to 0.125
- mr_filter: bfloat16 [128, 128], P('tp'), may hold values from -0.5 to 0.5
- out_weight_a: bfloat16 [2048, 2048], P('tp', 'ctx'), may hold values from -0.125 to 0.125
- norm_gain_b: float32 [2048], replicated, may hold values from 0.5 to 1.5
- in_weight_b: bfloat16 [3, 2048, 2048], P(None, 'ctx', 'tp'), may hold values from -0.125 to 0.125
- li_rate: float32 [128, 16], P('tp'), may hold values from 4.8828125e-05 to 0.0333333333
- li_residue: float32 [128, 16], P('tp'), may hold values from -3 to 3
- out_weight_b: bfloat16 [2048, 2048], P('tp', 'ctx'), may hold values from -0.125 to 0.125
Outputs:
- mixed: bfloat16 [2048, 2048], P('ctx', 'tp')
- gated_medium: bfloat16 [2048, 2048], P('tp', 'ctx')
- gated_long: bfloat16 [2048, 2048], P('tp', 'ctx')
The draws below stay inside these ranges and needn't reach their ends.
All inputs are finite; a program needn't handle non-finite values.
Results may differ from the reference program's by a relative error of at most 0.02.
Values may be sent and summed in bfloat16 or wider, within the bound.
A program may use at most 64 MiB of HBM per device.

```python
import math
import jax
import jax.numpy as jnp
from jax import lax

D = 2048
CH = 2048
GROUP = 16
TAPS = 128
MODES = 16
SEQ = 2048
GROUPS = 128


def draw_li_rate(key, part):
    share_key, slow_key, fast_key = jax.random.split(jax.random.fold_in(key, 7), 3)
    slow_share = 0.5
    picked = jax.random.uniform(share_key, (GROUPS, MODES)) < slow_share
    slow_rate = jnp.exp(jax.random.uniform(slow_key, (GROUPS, MODES), minval=math.log(0.1 / SEQ), maxval=math.log(2.0 / SEQ)))
    fast_rate = jnp.exp(jax.random.uniform(fast_key, (GROUPS, MODES), minval=math.log(1.0 / 50.0), maxval=math.log(1.0 / 30.0)))
    return jnp.where(picked, slow_rate, fast_rate).astype(jnp.float32)


def levels(rng, extent, pieces, least, top_value):
    def one(dim, shards_of):
        draws = jax.random.uniform(jax.random.fold_in(jax.random.fold_in(rng, 6), dim), (shards_of,), jnp.float32, least / len(pieces), top_value / len(pieces))
        return jnp.repeat(jnp.exp(draws), extent[dim] // shards_of).reshape((-1,) + (1,) * (len(extent) - dim - 1))

    level = one(*pieces[0])
    for cut in pieces[1:]:
        level = level * one(*cut)
    return level


def bell_draw(key, extent, deviation, limit, shards=(), held_as=jnp.bfloat16):
    array = deviation * jax.random.normal(key, extent, jnp.float32)
    if shards:
        array = array * levels(key, extent, shards, -0.22, 0.18)
    return jnp.clip(array, -limit, limit).astype(held_as)


def setup_inputs(seed: int = 0) -> dict:
    arg_keys = jax.random.split(jax.random.key(seed), 11)
    return {
        "hidden": bell_draw(arg_keys[0], (SEQ, D), 1.0, 6.0, ((0, 8), (1, 4))),
        "norm_gain_a": jnp.clip(1.0 + 0.1 * jax.random.normal(arg_keys[1], (D,), jnp.float32), 0.5, 1.5),
        "in_weight_a": bell_draw(arg_keys[2], (3, D, CH), D ** -0.5, 0.125, ((1, 8), (2, 4))),
        "mr_filter": bell_draw(arg_keys[3], (GROUPS, TAPS), TAPS ** -0.5, 0.5, ((0, 4),)),
        "out_weight_a": bell_draw(arg_keys[4], (CH, D), CH ** -0.5, 0.125, ((0, 4), (1, 8))),
        "norm_gain_b": jnp.clip(1.0 + 0.1 * jax.random.normal(arg_keys[5], (D,), jnp.float32), 0.5, 1.5),
        "in_weight_b": bell_draw(arg_keys[6], (3, D, CH), D ** -0.5, 0.125, ((1, 8), (2, 4))),
        "li_rate": draw_li_rate(jax.random.fold_in(arg_keys[10], 71), 0),
        "li_residue": bell_draw(arg_keys[8], (GROUPS, MODES), 0.5, 3.0, ((0, 4),), jnp.float32),
        "out_weight_b": bell_draw(arg_keys[9], (CH, D), CH ** -0.5, 0.125, ((0, 4), (1, 8))),
    }


def normalize(values, gain):
    widened = values.astype(jnp.float32)
    factor = lax.rsqrt(lax.optimization_barrier(jnp.mean(widened * widened, axis=1, keepdims=True)) + 1e-06)
    return (widened * factor * gain).astype(jnp.bfloat16)

def layer_inputs(values, gain, weight):
    normed = normalize(values, gain)
    first = jnp.dot(normed, weight[0], preferred_element_type=jnp.float32)
    gating = jnp.dot(normed, weight[1], preferred_element_type=jnp.float32)
    second = jnp.dot(normed, weight[2], preferred_element_type=jnp.float32)
    return (gating, (first * second).astype(jnp.bfloat16))

def causal_conv(values, filters):
    length = values.shape[0]
    padded_len = 2 * length
    grouped = values.reshape(length, GROUPS, GROUP).transpose(1, 0, 2)

    def one_group(pair):
        group_values, group_filter = pair
        spectrum = jnp.fft.rfft(group_values, n=padded_len, axis=0)
        response = jnp.fft.rfft(group_filter, n=padded_len)
        return jnp.fft.irfft(spectrum * response[:, None], n=padded_len, axis=0)[:length].astype(jnp.float32)
    result = lax.map(one_group, (grouped, filters))
    return result.transpose(1, 0, 2).reshape(length, GROUPS * GROUP)

def reference(hidden, norm_gain_a, in_weight_a, mr_filter, out_weight_a, norm_gain_b, in_weight_b, li_rate, li_residue, out_weight_b):
    gate_first, medium_in = layer_inputs(hidden, norm_gain_a, in_weight_a)
    medium = causal_conv(medium_in.astype(jnp.float32), mr_filter.astype(jnp.float32))
    gated_medium = (gate_first * medium).astype(jnp.bfloat16)
    after_a = (hidden.astype(jnp.float32) + jnp.dot(gated_medium, out_weight_a, preferred_element_type=jnp.float32)).astype(jnp.bfloat16)
    gate_second, long_in = layer_inputs(after_a, norm_gain_b, in_weight_b)
    offsets = jnp.arange(SEQ, dtype=jnp.float32)
    mode_weight = li_residue * jnp.sqrt(2.0 * li_rate)
    long_filter = lax.optimization_barrier(jnp.sum(mode_weight[:, :, None] * jnp.exp(-li_rate[:, :, None] * offsets), axis=1))
    long_out = causal_conv(long_in.astype(jnp.float32), long_filter)
    gated_long = (gate_second * long_out).astype(jnp.bfloat16)
    mixed = (after_a.astype(jnp.float32) + jnp.dot(gated_long, out_weight_b, preferred_element_type=jnp.float32)).astype(jnp.bfloat16)
    return (mixed, gated_medium.T, gated_long.T)
```

```python
import functools

import jax
import jax.numpy as jnp
from jax import lax
from jax.experimental import pallas as pl
from jax.experimental.pallas import tpu as pltpu
from jax.sharding import PartitionSpec as P

LANES = 128
MESH = pl.DeviceIdType.MESH
f32 = jnp.float32
bf16 = jnp.bfloat16
highest = lax.Precision.HIGHEST


def dot(a, b, precision=None):
    return lax.dot_general(
        a, b, (((1,), (0,)), ((), ())), precision=precision, preferred_element_type=f32
    )


def iota(shape, dim):
    return lax.broadcasted_iota(jnp.int32, shape, dim)


def kernel(
    n,
    ntp,
    hidden,
    gain_a,
    win_a,
    mr_filter,
    wout_a,
    gain_b,
    win_b,
    rate,
    residue,
    mode_rows,
    rate_mc,
    wout_b,
    mixed,
    gated_a_out,
    gated_b_out,
    wa,
    oa,
    wb,
    ob,
    hbuf,
    abuf,
    normed,
    proj,
    xin,
    halo,
    conv,
    gated,
    part,
    landed,
    states,
    toep_a,
    toep_b,
    rows_a,
    rows_b,
    to_end,
    from_start,
    ring_send,
    ring_recv,
    tp_send,
    tp_recv,
    state_send,
    state_recv,
    halo_sems,
    local_sems,
):
    me = lax.axis_index("ctx")
    mytp = lax.axis_index("tp")
    tokens, width = hidden.shape
    channels = win_a.shape[2]
    dn = win_a.shape[1]
    on = wout_a.shape[1]
    features = width * ntp
    groups, taps = mr_filter.shape
    modes = rate.shape[1]
    per = channels // groups
    tile_groups = LANES // per
    tiles = channels // LANES
    blocks = tokens // taps
    half_ring = n // 2

    odd = lax.rem(me, 2)
    pos = (1 - odd) * lax.div(me, 2) + odd * (n - 1 - lax.div(me, 2))

    def index_at(position):
        p = lax.rem(position + 2 * n, n)
        back = lax.div(p, half_ring)
        return (1 - back) * (2 * p) + back * (2 * (n - 1 - p) + 1)

    neighbour = (index_at(pos + 1), index_at(pos - 1))

    barrier = pltpu.get_barrier_semaphore()

    def greet_ctx(off, carry):
        pl.semaphore_signal(
            barrier, inc=1, device_id={"ctx": lax.rem(me + off, n)}, device_id_type=MESH
        )
        return carry

    lax.fori_loop(1, n, greet_ctx, 0)
    for off in range(1, ntp):
        pl.semaphore_signal(
            barrier, inc=1, device_id={"tp": lax.rem(mytp + off, ntp)}, device_id_type=MESH
        )

    def in_rows(ref, owner, way):
        half = dn // 2
        return ref.at[:, pl.ds(pl.multiple_of(owner * dn + way * half, half), half), :]

    def out_rows(ref, owner, way):
        half = channels // 2
        return ref.at[owner, pl.ds(way * half, half), :]

    streams = (
        (win_a, wa, in_rows, lambda way: win_a.at[:, pl.ds(way * (dn // 2), dn // 2), :]),
        (wout_a, oa, out_rows, lambda way: wout_a.at[pl.ds(way * (channels // 2), channels // 2), :]),
        (win_b, wb, in_rows, lambda way: win_b.at[:, pl.ds(way * (dn // 2), dn // 2), :]),
        (wout_b, ob, out_rows, lambda way: wout_b.at[pl.ds(way * (channels // 2), channels // 2), :]),
    )

    def ring_copy(stream, way, step, first=False):
        source, buffer, rows, own = streams[stream]
        owner = index_at(pos - step) if way == 0 else index_at(pos + step)
        return pltpu.make_async_remote_copy(
            src_ref=own(way) if first else rows(buffer, owner, way),
            dst_ref=rows(buffer, owner, way),
            send_sem=ring_send.at[stream, way, step],
            recv_sem=ring_recv.at[stream, way, step],
            device_id={"ctx": neighbour[way]},
            device_id_type=MESH,
        )

    def arrival(stream, way, step):
        source, buffer, rows, own = streams[stream]
        owner = index_at(pos - step - 1) if way == 0 else index_at(pos + step + 1)
        return pltpu.make_async_remote_copy(
            src_ref=rows(buffer, owner, way),
            dst_ref=rows(buffer, owner, way),
            send_sem=ring_send.at[stream, way, step],
            recv_sem=ring_recv.at[stream, way, step],
            device_id={"ctx": neighbour[way]},
            device_id_type=MESH,
        )

    def ring_start(stream):
        for way in (0, 1):
            ring_copy(stream, way, 0, True).start()

    def pump(which, low, high):
        def body(step, carry):
            for stream in which:
                for way in (0, 1):
                    arrival(stream, way, step - 1).wait_recv()
                    ring_copy(stream, way, step).start()
            return carry

        if high > low:
            lax.fori_loop(low, high, body, 0)

    def ring_end(stream):
        for way in (0, 1):
            arrival(stream, way, n - 2).wait_recv()

    def own_copy(stream):
        if stream in (0, 2):
            source, buffer = streams[stream][:2]
            target = buffer.at[:, pl.ds(pl.multiple_of(me * dn, dn), dn), :]
        else:
            source, buffer = streams[stream][:2]
            target = buffer.at[me]
        return pltpu.make_async_copy(source, target, local_sems.at[stream])

    def tp_copy(use, off, src, dst):
        return pltpu.make_async_remote_copy(
            src_ref=src,
            dst_ref=dst,
            send_sem=tp_send.at[use, off - 1],
            recv_sem=tp_recv.at[use, off - 1],
            device_id={"tp": lax.rem(mytp + off, ntp)},
            device_id_type=MESH,
        )

    def gather_start(use, buffer):
        for off in range(1, ntp):
            tp_copy(use, off, buffer.at[mytp], buffer.at[mytp]).start()

    def gather_wait(use, buffer):
        for off in range(1, ntp):
            sender = lax.rem(mytp - off + ntp, ntp)
            tp_copy(use, off, buffer.at[sender], buffer.at[sender]).wait_recv()

    def gather_sent(use, buffer):
        for off in range(1, ntp):
            tp_copy(use, off, buffer.at[mytp], buffer.at[mytp]).wait_send()

    def normalize(buffer, gain):
        total = jnp.zeros((tokens, 1), f32)
        for block in range(ntp):
            wide = buffer[block].astype(f32)
            total = total + jnp.sum(wide * wide, axis=1, keepdims=True)
        factor = lax.rsqrt(total / features + 1e-06)
        for block in range(ntp):
            at = slice(block * width, (block + 1) * width)
            normed[:, at] = (buffer[block].astype(f32) * factor * gain[:, at]).astype(bf16)

    def in_project(weight):
        span = min(256, channels)

        def body(k, carry):
            for at in range(0, channels, span):
                proj[k, :, at : at + span] = dot(normed[...], weight[k, :, at : at + span])
            return carry

        lax.fori_loop(0, 3, body, 0)
        xin[...] = (proj[0] * proj[2]).astype(bf16)

    def out_block(buffer, p, j):
        return dot(gated[...], buffer[p * (width // on) + j])

    def scatter_start(which, use, buffer):
        for off in range(1, ntp):
            p = lax.rem(mytp + off, ntp)
            for j in range(width // on):
                part[which, off - 1, :, j * on : (j + 1) * on] = out_block(buffer, p, j).astype(bf16)
            tp_copy(use, off, part.at[which, off - 1], landed.at[which, off - 1]).start()
        for j in range(width // on):
            proj[0, :, j * on : (j + 1) * on] = out_block(buffer, mytp, j)

    def scatter_end(which, use, base):
        total = base.astype(f32) + proj[0, :, :width]
        for off in range(1, ntp):
            tp_copy(use, off, part.at[which, off - 1], landed.at[which, off - 1]).wait_recv()
            total = total + landed[which, off - 1].astype(f32)
        return total.astype(bf16)

    def scatter_sent(which, use):
        for off in range(1, ntp):
            tp_copy(use, off, part.at[which, off - 1], landed.at[which, off - 1]).wait_send()

    def lanes(q):
        return pl.ds(pl.multiple_of(q * LANES, LANES), LANES)

    hbuf[mytp] = hidden[...]
    for stream in range(4):
        own_copy(stream).start()
    pl.semaphore_wait(barrier, (n - 1) + (ntp - 1))

    gather_start(0, hbuf)
    ring_start(0)
    ring_start(1)

    flip = (lax.rem(iota((taps, taps), 0) + iota((taps, taps), 1), taps) == 0).astype(bf16)
    rows_a[...] = dot(mr_filter[...], flip)
    lag = lax.rem(tokens - iota((groups, tokens), 1), tokens).astype(f32)
    impulse = jnp.zeros((groups, tokens), f32)
    for m in range(modes):
        r = rate[:, m : m + 1]
        impulse = impulse + residue[:, m : m + 1] * jnp.sqrt(2.0 * r) * jnp.exp(-r * lag)
    rows_b[...] = impulse

    def build(g, carry):
        row = jnp.broadcast_to(rows_a[pl.ds(g, 1), :], (taps, taps))
        turned = pltpu.roll(row, 0, 1, stride=1, stride_axis=0)
        below = iota((taps, taps), 1) <= iota((taps, taps), 0)
        toep_a[g, :, :taps] = jnp.where(below, 0.0, turned).astype(bf16)
        toep_a[g, :, taps:] = jnp.where(below, turned, 0.0).astype(bf16)
        row = jnp.broadcast_to(rows_b[pl.ds(g, 1), :], (tokens, tokens))
        turned = pltpu.roll(row, 0, 1, stride=1, stride_axis=0)
        below = iota((tokens, tokens), 1) <= iota((tokens, tokens), 0)
        toep_b[g] = jnp.where(below, turned, 0.0).astype(bf16)
        return carry

    lax.fori_loop(0, groups, build, 0)
    pump((0, 1), 1, min(2, n - 1))

    rate_row = mode_rows[0:1, :]
    weight_row = mode_rows[1:2, :] * jnp.sqrt(2.0 * rate_row)
    position = iota((tokens, groups * modes), 0).astype(f32)
    from_start[...] = weight_row * jnp.exp(-rate_row * (position + 1.0))
    to_end[...] = jnp.exp(-rate_row * (tokens - 1.0 - position)).T

    gather_wait(0, hbuf)
    normalize(hbuf, gain_a)
    pump((0, 1), 2, n - 1)
    own_copy(0).wait()
    own_copy(1).wait()
    ring_start(2)
    ring_start(3)
    ring_end(0)

    in_project(wa)
    onward = pltpu.make_async_remote_copy(
        src_ref=xin.at[pl.ds(tokens - taps, taps), :],
        dst_ref=halo,
        send_sem=halo_sems.at[0],
        recv_sem=halo_sems.at[1],
        device_id={"ctx": lax.rem(me + 1, n)},
        device_id_type=MESH,
    )
    onward.start()
    ring_end(1)
    steps = [1 + (n - 2) * k // 4 for k in range(5)]
    pump((2, 3), steps[0], steps[1])
    onward.wait()

    def medium_tile(q, carry):
        at = lanes(q)
        before = halo[:, at]
        before = jnp.where(me > 0, before, jnp.zeros_like(before))
        here = [xin[b * taps : (b + 1) * taps, at] for b in range(blocks)]
        early = [before] + here[:-1]
        window = jnp.concatenate(
            [jnp.concatenate(early, axis=1), jnp.concatenate(here, axis=1)], axis=0
        )
        group_of = lax.div(lax.rem(iota((taps, blocks * LANES), 1), LANES), per)
        total = jnp.zeros((taps, blocks * LANES), f32)
        for g in range(tile_groups):
            total = jnp.where(group_of == g, dot(toep_a[q * tile_groups + g], window), total)
        for b in range(blocks):
            conv[b * taps : (b + 1) * taps, at] = total[:, b * LANES : (b + 1) * LANES]
        return carry

    lax.fori_loop(0, tiles, medium_tile, 0)
    product = proj[1] * conv[...]
    gated[...] = product.astype(bf16)
    gated_a_out[...] = product.T.astype(bf16)
    scatter_start(0, 1, oa)
    pump((2, 3), steps[1], steps[2])
    after = scatter_end(0, 1, hidden[...])
    abuf[mytp] = after
    gather_start(2, abuf)
    pump((2, 3), steps[2], steps[3])
    gather_wait(2, abuf)
    normalize(abuf, gain_b)
    pump((2, 3), steps[3], steps[4])
    own_copy(2).wait()
    own_copy(3).wait()
    ring_end(2)

    in_project(wb)

    def same_group(shape):
        return lax.div(iota(shape, 0), modes) == lax.div(iota(shape, 1), per)

    side = tile_groups * modes
    for q in range(tiles):
        at = slice(q * LANES, (q + 1) * LANES)
        ends = dot(to_end[q * side : (q + 1) * side, :], xin[:, at].astype(f32), highest)
        ends = jnp.where(same_group((side, LANES)), ends, 0.0)
        total = ends[0:modes]
        for g in range(1, tile_groups):
            total = total + ends[g * modes : (g + 1) * modes]
        states[me, :, at] = total

    def state_copy(off, slot, to):
        return pltpu.make_async_remote_copy(
            src_ref=states.at[slot],
            dst_ref=states.at[slot],
            send_sem=state_send.at[off - 1],
            recv_sem=state_recv.at[off - 1],
            device_id={"ctx": to},
            device_id_type=MESH,
        )

    def state_start(off, carry):
        state_copy(off, me, lax.rem(me + off, n)).start()
        return carry

    lax.fori_loop(1, n, state_start, 0)

    def long_tile(q, carry):
        at = lanes(q)
        values = xin[:, at]
        group_of = lax.div(iota((tokens, LANES), 1), per)
        total = jnp.zeros((tokens, LANES), f32)
        for g in range(tile_groups):
            total = jnp.where(group_of == g, dot(toep_b[q * tile_groups + g], values), total)
        conv[:, at] = total
        return carry

    lax.fori_loop(0, tiles, long_tile, 0)

    def state_wait(off, carry):
        state_copy(off, lax.rem(me - off + n, n), lax.rem(me + off, n)).wait_recv()
        return carry

    lax.fori_loop(1, n, state_wait, 0)

    def state_add(j, total):
        gap = jnp.maximum(me - 1 - j, 0).astype(f32) * tokens
        term = jnp.exp(-rate_mc[...] * gap) * states[j]
        return total + jnp.where(j < me, term, jnp.zeros_like(term))

    entering = lax.fori_loop(0, n, state_add, jnp.zeros((modes, channels), f32))
    for q in range(tiles):
        at = slice(q * LANES, (q + 1) * LANES)
        spread = jnp.concatenate([entering[:, at]] * tile_groups, axis=0)
        spread = jnp.where(same_group((side, LANES)), spread, 0.0)
        conv[:, at] += dot(from_start[:, q * side : (q + 1) * side], spread, highest)
    product = proj[1] * conv[...]
    gated[...] = product.astype(bf16)
    ring_end(3)
    scatter_start(1, 3, ob)
    gated_b_out[...] = product.T.astype(bf16)
    mixed[...] = scatter_end(1, 3, abuf[mytp])

    gather_sent(0, hbuf)
    gather_sent(2, abuf)
    scatter_sent(0, 1)
    scatter_sent(1, 3)

    def state_sent(off, carry):
        state_copy(off, me, lax.rem(me + off, n)).wait_send()
        return carry

    lax.fori_loop(1, n, state_sent, 0)

    def ring_sent(step, carry):
        for stream in range(4):
            for way in (0, 1):
                ring_copy(stream, way, step).wait_send()
        return carry

    lax.fori_loop(0, n - 1, ring_sent, 0)


def per_device(
    n,
    ntp,
    hidden,
    norm_gain_a,
    in_weight_a,
    mr_filter,
    out_weight_a,
    norm_gain_b,
    in_weight_b,
    li_rate,
    li_residue,
    out_weight_b,
):
    tokens, width = hidden.shape
    dn, channels = in_weight_a.shape[1:]
    on = out_weight_a.shape[1]
    features = width * ntp
    groups, taps = mr_filter.shape
    modes = li_rate.shape[1]
    mode_rows = jnp.stack([li_rate.reshape(-1), li_residue.reshape(-1)])
    rate_mc = jnp.repeat(li_rate.T, channels // groups, axis=1)
    vmem = pl.BlockSpec(memory_space=pltpu.VMEM)
    anywhere = pl.BlockSpec(memory_space=pl.ANY)
    flops = 2 * tokens * features * channels * 8 + 2 * tokens * channels * (tokens + 2 * taps) * 8
    return pl.pallas_call(
        functools.partial(kernel, n, ntp),
        out_shape=(
            jax.ShapeDtypeStruct((tokens, width), bf16),
            jax.ShapeDtypeStruct((channels, tokens), bf16),
            jax.ShapeDtypeStruct((channels, tokens), bf16),
        ),
        in_specs=[vmem, vmem, anywhere, vmem, anywhere, vmem, anywhere, vmem, vmem, vmem, vmem, anywhere],
        out_specs=(vmem, vmem, vmem),
        scratch_shapes=[
            pltpu.VMEM((3, features, channels), bf16),
            pltpu.VMEM((n, channels, on), bf16),
            pltpu.VMEM((3, features, channels), bf16),
            pltpu.VMEM((n, channels, on), bf16),
            pltpu.VMEM((ntp, tokens, width), bf16),
            pltpu.VMEM((ntp, tokens, width), bf16),
            pltpu.VMEM((tokens, features), bf16),
            pltpu.VMEM((3, tokens, channels), f32),
            pltpu.VMEM((tokens, channels), bf16),
            pltpu.VMEM((taps, channels), bf16),
            pltpu.VMEM((tokens, channels), f32),
            pltpu.VMEM((tokens, channels), bf16),
            pltpu.VMEM((2, ntp - 1, tokens, width), bf16),
            pltpu.VMEM((2, ntp - 1, tokens, width), bf16),
            pltpu.VMEM((n, modes, channels), f32),
            pltpu.VMEM((groups, taps, 2 * taps), bf16),
            pltpu.VMEM((groups, tokens, tokens), bf16),
            pltpu.VMEM((groups, taps), f32),
            pltpu.VMEM((groups, tokens), f32),
            pltpu.VMEM((groups * modes, tokens), f32),
            pltpu.VMEM((tokens, groups * modes), f32),
            pltpu.SemaphoreType.DMA((4, 2, n - 1)),
            pltpu.SemaphoreType.DMA((4, 2, n - 1)),
            pltpu.SemaphoreType.DMA((4, ntp - 1)),
            pltpu.SemaphoreType.DMA((4, ntp - 1)),
            pltpu.SemaphoreType.DMA((n - 1,)),
            pltpu.SemaphoreType.DMA((n - 1,)),
            pltpu.SemaphoreType.DMA((2,)),
            pltpu.SemaphoreType.DMA((4,)),
        ],
        cost_estimate=pl.CostEstimate(flops=flops, bytes_accessed=32 * 1024 * 1024, transcendentals=0),
        compiler_params=pltpu.CompilerParams(
            collective_id=0, has_side_effects=True, vmem_limit_bytes=56 * 1024 * 1024
        ),
    )(
        hidden,
        norm_gain_a.reshape(1, -1),
        in_weight_a,
        mr_filter,
        out_weight_a,
        norm_gain_b.reshape(1, -1),
        in_weight_b,
        li_rate,
        li_residue,
        mode_rows,
        rate_mc,
        out_weight_b,
    )


def solution(mesh):
    in_specs = (
        P("ctx", "tp"),
        P(),
        P(None, "ctx", "tp"),
        P("tp", None),
        P("tp", "ctx"),
        P(),
        P(None, "ctx", "tp"),
        P("tp", None),
        P("tp", None),
        P("tp", "ctx"),
    )
    out_specs = (P("ctx", "tp"), P("tp", "ctx"), P("tp", "ctx"))
    return jax.shard_map(
        functools.partial(per_device, mesh.shape["ctx"], mesh.shape["tp"]),
        mesh=mesh,
        in_specs=in_specs,
        out_specs=out_specs,
        check_vma=False,
    )
```

```python
import functools

import jax
import jax.numpy as jnp
from jax import lax
from jax.experimental import pallas as pl
from jax.experimental.pallas import tpu as pltpu
from jax.sharding import PartitionSpec as P

LANES = 128
MESH = pl.DeviceIdType.MESH
f32 = jnp.float32
bf16 = jnp.bfloat16
highest = lax.Precision.HIGHEST


def dot(a, b, precision=None):
    return lax.dot_general(
        a, b, (((1,), (0,)), ((), ())), precision=precision, preferred_element_type=f32
    )


def iota(shape, dim):
    return lax.broadcasted_iota(jnp.int32, shape, dim)


def kernel(
    n,
    ntp,
    hidden,
    gain_a,
    win_a,
    mr_filter,
    wout_a,
    gain_b,
    win_b,
    rate,
    residue,
    mode_rows,
    rate_mc,
    wout_b,
    mixed,
    gated_a_out,
    gated_b_out,
    wa,
    oa,
    wb,
    ob,
    hbuf,
    abuf,
    normed,
    proj,
    xin,
    halos,
    conv,
    gated,
    part,
    from_core,
    core_sum,
    from_first,
    first_sum,
    from_last,
    turned,
    turned_out,
    states,
    toep_a,
    toep_b,
    rows_a,
    rows_b,
    to_end,
    from_start,
    line_send,
    line_recv,
    cross_send,
    cross_recv,
    swap_send,
    swap_recv,
    state_send,
    state_recv,
    halo_send,
    halo_recv,
    local_sems,
):
    me = lax.axis_index("ctx")
    mytp = lax.axis_index("tp")
    tokens, width = hidden.shape
    all_channels = win_a.shape[2]
    channels = all_channels // 2
    dn = win_a.shape[1]
    on = wout_a.shape[1]
    features = width * ntp
    all_groups, taps = mr_filter.shape
    groups = all_groups // 2
    modes = rate.shape[1]
    per = channels // groups
    tile_groups = LANES // per
    tiles = channels // LANES
    blocks = tokens // taps
    depth = n // 2
    rows2 = tokens // 2

    z, y = lax.div(me, 2), lax.rem(me, 2)
    lo = lax.rem(z, 2)
    pair = lax.div(z, 2)
    x, core = lax.div(mytp, 2), lax.rem(mytp, 2)
    core_peer = {"tp": x * 2 + 1 - core}
    x_peer = {"tp": (1 - x) * 2 + core}
    z_peer = {"ctx": (z + 1 - 2 * lo) * 2 + y}
    y_peer = {"ctx": z * 2 + 1 - y}

    barrier = pltpu.get_barrier_semaphore()

    def greet_ctx(off, carry):
        pl.semaphore_signal(
            barrier, inc=1, device_id={"ctx": lax.rem(me + off, n)}, device_id_type=MESH
        )
        return carry

    lax.fori_loop(1, n, greet_ctx, 0)
    for peer in (core_peer, x_peer):
        pl.semaphore_signal(barrier, inc=1, device_id=peer, device_id_type=MESH)

    def remote(src, dst, send, recv, peer):
        return pltpu.make_async_remote_copy(
            src_ref=src,
            dst_ref=dst,
            send_sem=send,
            recv_sem=recv,
            device_id=peer,
            device_id_type=MESH,
        )

    streams = ((win_a, wa), (wout_a, oa), (win_b, wb), (wout_b, ob))

    def slot(stream, h, owner):
        buffer = streams[stream][1]
        if stream in (0, 2):
            return buffer.at[h, :, pl.ds(pl.multiple_of(owner * dn, dn), dn), :]
        return buffer.at[h, owner]

    def own(stream, h):
        source = streams[stream][0]
        at = pl.ds(pl.multiple_of(h * channels, channels), channels)
        return source.at[:, :, at] if stream in (0, 2) else source.at[at, :]

    def along(way):
        return (z, 1) if way == 0 else (depth - 1 - z, -1)

    def line_copy(stream, way, kind, step, first=False):
        zz, d = along(way)
        h = 1 - lo if kind == 0 else lo
        owner = (z - d * step) * 2 + y
        return remote(
            own(stream, h) if first else slot(stream, h, owner),
            slot(stream, h, owner),
            line_send.at[stream, way, kind, step],
            line_recv.at[stream, way, kind, step],
            {"ctx": (z + d) * 2 + y},
        )

    def line_arrival(stream, way, kind, step):
        zz, d = along(way)
        h = lo if kind == 0 else 1 - lo
        owner = (z - d * (step + 1)) * 2 + y
        here = slot(stream, h, owner)
        return remote(
            here,
            here,
            line_send.at[stream, way, kind, step],
            line_recv.at[stream, way, kind, step],
            {"ctx": (z - d) * 2 + y},
        )

    def cross_copy(stream, way, step, side):
        zz, d = along(way)
        owner = (z - d * step) * 2 + side
        here = slot(stream, lo, owner)
        return remote(
            here, here, cross_send.at[stream, way, step], cross_recv.at[stream, way, step], y_peer
        )

    def cross_own(stream):
        return remote(
            own(stream, lo),
            slot(stream, lo, me),
            cross_send.at[stream, 0, 0],
            cross_recv.at[stream, 0, 0],
            y_peer,
        )

    def start(stream):
        for way in (0, 1):
            zz, d = along(way)

            @pl.when(zz + 1 < depth)
            def near():
                line_copy(stream, way, 0, 0, True).start()

        for way in (0, 1):
            zz, d = along(way)

            @pl.when(zz + 2 < depth)
            def through():
                line_copy(stream, way, 1, 0, True).start()

        cross_own(stream).start()

    def pump_step(stream, step):
        for way in (0, 1):
            zz, d = along(way)

            @pl.when(zz - step >= 0)
            def arrived():
                line_arrival(stream, way, 0, step - 1).wait_recv()

                @pl.when(zz + 2 < depth)
                def through():
                    line_copy(stream, way, 1, step).start()

                cross_copy(stream, way, step, y).start()

                @pl.when(zz + 1 < depth)
                def near():
                    line_arrival(stream, way, 1, step - 1).wait_recv()
                    line_copy(stream, way, 0, step).start()

    def pump(stream, low, high):
        def body(step, carry):
            pump_step(stream, step)
            return carry

        if high > low:
            lax.fori_loop(low, high, body, 0)

    def finish(stream):
        cross_copy(stream, 0, 0, 1 - y).wait_recv()

        def body(step, carry):
            for way in (0, 1):
                zz, d = along(way)

                @pl.when(zz - step >= 0)
                def arrived():
                    cross_copy(stream, way, step, 1 - y).wait_recv()

            return carry

        lax.fori_loop(1, depth, body, 0)
        own_copy(stream).wait()

    def all_sent(stream):
        cross_own(stream).wait_send()

        def body(step, carry):
            for way in (0, 1):
                zz, d = along(way)

                @pl.when(zz - step >= 0)
                def passed():
                    @pl.when(zz + 1 < depth)
                    def near():
                        line_copy(stream, way, 0, step).wait_send()

                    @pl.when(zz + 2 < depth)
                    def through():
                        line_copy(stream, way, 1, step).wait_send()

                    @pl.when(step > 0)
                    def crossed():
                        cross_copy(stream, way, step, y).wait_send()

            return carry

        lax.fori_loop(0, depth, body, 0)

    def own_copy(stream):
        return pltpu.make_async_copy(own(stream, lo), slot(stream, lo, me), local_sems.at[stream])

    upper, lower = pl.ds(0, rows2), pl.ds(rows2, rows2)

    def swap(use, step, src, dst, peer):
        return remote(src, dst, swap_send.at[use, step], swap_recv.at[use, step], peer)

    def gather_moves(use, buffer):
        def move(step, ref_out, ref_in, peer):
            return (swap(use, step, ref_out, ref_out, peer), swap(use, step, ref_in, ref_in, peer))

        return (
            move(0, buffer.at[lo, x, core, upper], buffer.at[1 - lo, x, core, upper], z_peer),
            move(1, buffer.at[lo, x, core, lower], buffer.at[lo, 1 - x, core, lower], x_peer),
            move(2, buffer.at[:, x, core, upper], buffer.at[:, 1 - x, core, upper], x_peer),
            move(3, buffer.at[lo, :, core, lower], buffer.at[1 - lo, :, core, lower], z_peer),
            move(4, buffer.at[:, :, core], buffer.at[:, :, 1 - core], core_peer),
        )

    def gather_first(use, buffer):
        moves = gather_moves(use, buffer)
        moves[0][0].start()
        moves[1][0].start()

    def gather_second(use, buffer):
        moves = gather_moves(use, buffer)
        moves[0][1].wait_recv()
        moves[2][0].start()
        moves[1][1].wait_recv()
        moves[3][0].start()

    def gather_third(use, buffer):
        moves = gather_moves(use, buffer)
        moves[2][1].wait_recv()
        moves[3][1].wait_recv()
        moves[4][0].start()

    def gather_end(use, buffer):
        moves = gather_moves(use, buffer)
        moves[4][1].wait_recv()
        for out, into in moves:
            out.wait_send()

    def normalize(buffer, gain):
        for b in range(2):
            total = jnp.zeros((tokens, 1), f32)
            for block in range(ntp):
                wide = buffer[b, block // 2, block % 2].astype(f32)
                total = total + jnp.sum(wide * wide, axis=1, keepdims=True)
            factor = lax.rsqrt(total / features + 1e-06)
            for block in range(ntp):
                at = slice(block * width, (block + 1) * width)
                wide = buffer[b, block // 2, block % 2].astype(f32)
                normed[b * tokens : (b + 1) * tokens, at] = (wide * factor * gain[:, at]).astype(bf16)

    def in_project(weight):
        def body(k, carry):
            proj[k] = dot(normed[...], weight[lo, k])
            return carry

        lax.fori_loop(0, 3, body, 0)
        xin[...] = (proj[0] * proj[2]).astype(bf16)

    def out_blocks(buffer, c):
        def body(xx, carry):
            for j in range(width // on):
                block = dot(gated[...], buffer[lo, (xx * 2 + c) * (width // on) + j]).astype(bf16)
                for b in range(2):
                    part[b, xx, c, :, j * on : (j + 1) * on] = block[b * tokens : (b + 1) * tokens]
            return carry

        lax.fori_loop(0, 2, body, 0)

    def scatter_moves(which):
        use = 2 + which
        return (
            swap(use, 0, part.at[:, :, 1 - core], from_core.at[which], core_peer),
            swap(use, 1, core_sum.at[1 - lo, :, upper], from_first.at[which, 0], z_peer),
            swap(use, 2, core_sum.at[:, 1 - x, lower], from_first.at[which, 1], x_peer),
            swap(use, 3, first_sum.at[0, 1 - x], from_last.at[which, 0], x_peer),
            swap(use, 4, first_sum.at[1, 1 - lo], from_last.at[which, 1], z_peer),
        )

    def scatter_first(which, buffer):
        moves = scatter_moves(which)
        out_blocks(buffer, 1 - core)
        moves[0].start()
        out_blocks(buffer, core)

    def scatter_second(which):
        moves = scatter_moves(which)
        moves[0].wait_recv()

        def add(b, xx, at):
            core_sum[b, xx, at] = (
                part[b, xx, core, at].astype(f32) + from_core[which, b, xx, at].astype(f32)
            ).astype(bf16)

        for xx in range(2):
            add(1 - lo, xx, upper)
        moves[1].start()
        for b in range(2):
            add(b, 1 - x, lower)
        moves[2].start()
        for xx in range(2):
            add(lo, xx, upper)
        for b in range(2):
            add(b, x, lower)

    def scatter_third(which):
        moves = scatter_moves(which)
        moves[1].wait_recv()
        for xx in range(2):
            first_sum[0, xx] = (
                core_sum[lo, xx, upper].astype(f32) + from_first[which, 0, xx].astype(f32)
            ).astype(bf16)
        moves[3].start()
        moves[2].wait_recv()
        for b in range(2):
            first_sum[1, b] = (
                core_sum[b, x, lower].astype(f32) + from_first[which, 1, b].astype(f32)
            ).astype(bf16)
        moves[4].start()

    def scatter_end(which, base, out):
        moves = scatter_moves(which)
        moves[3].wait_recv()
        out[upper] = (
            base[upper].astype(f32) + first_sum[0, x].astype(f32) + from_last[which, 0].astype(f32)
        ).astype(bf16)
        moves[4].wait_recv()
        out[lower] = (
            base[lower].astype(f32) + first_sum[1, lo].astype(f32) + from_last[which, 1].astype(f32)
        ).astype(bf16)
        for move in moves:
            move.wait_send()

    def give_move(which):
        return swap(
            4, which, turned.at[which], turned_out.at[which, pl.ds(pl.multiple_of(lo * channels, channels), channels)], z_peer
        )

    def give_back(which, product):
        flat = product.T.astype(bf16)
        at = pl.ds(pl.multiple_of(lo * channels, channels), channels)
        own_block = jnp.where(lo == 0, flat[:, :tokens], flat[:, tokens:])
        other = jnp.where(lo == 0, flat[:, tokens:], flat[:, :tokens])
        turned[which] = other
        turned_out[which, at] = own_block
        give_move(which).start()

    def give_end(which):
        give_move(which).wait_send()
        arriving = turned_out.at[which, pl.ds(pl.multiple_of((1 - lo) * channels, channels), channels)]
        swap(4, which, turned.at[which], arriving, z_peer).wait_recv()

    def lanes(q):
        return pl.ds(pl.multiple_of(q * LANES, LANES), LANES)

    hbuf[lo, x, core] = hidden[...]
    for stream in range(4):
        own_copy(stream).start()
    pl.semaphore_wait(barrier, (n - 1) + 2)

    gather_first(0, hbuf)
    start(0)
    start(1)

    flip = (lax.rem(iota((taps, taps), 0) + iota((taps, taps), 1), taps) == 0).astype(bf16)
    rows_a[...] = dot(mr_filter[...], flip)
    lag = lax.rem(tokens - iota((all_groups, tokens), 1), tokens).astype(f32)
    impulse = jnp.zeros((all_groups, tokens), f32)
    for m in range(modes):
        r = rate[:, m : m + 1]
        impulse = impulse + residue[:, m : m + 1] * jnp.sqrt(2.0 * r) * jnp.exp(-r * lag)
    rows_b[...] = impulse

    def build_a(g, carry):
        row = jnp.broadcast_to(rows_a[pl.ds(lo * groups + g, 1), :], (taps, taps))
        rolled = pltpu.roll(row, 0, 1, stride=1, stride_axis=0)
        below = iota((taps, taps), 1) <= iota((taps, taps), 0)
        toep_a[g, :, :taps] = jnp.where(below, 0.0, rolled).astype(bf16)
        toep_a[g, :, taps:] = jnp.where(below, rolled, 0.0).astype(bf16)
        return carry

    def build_b(g, carry):
        row = jnp.broadcast_to(rows_b[pl.ds(lo * groups + g, 1), :], (tokens, tokens))
        rolled = pltpu.roll(row, 0, 1, stride=1, stride_axis=0)
        below = iota((tokens, tokens), 1) <= iota((tokens, tokens), 0)
        toep_b[g] = jnp.where(below, rolled, 0.0).astype(bf16)
        return carry

    lax.fori_loop(0, groups, build_a, 0)
    gather_second(0, hbuf)
    lax.fori_loop(0, groups, build_b, 0)
    gather_third(0, hbuf)

    mode_lanes = pl.ds(pl.multiple_of(lo * groups * modes, LANES), groups * modes)
    rate_row = mode_rows[0:1, mode_lanes]
    weight_row = mode_rows[1:2, mode_lanes] * jnp.sqrt(2.0 * rate_row)
    position = iota((tokens, groups * modes), 0).astype(f32)
    from_start[...] = weight_row * jnp.exp(-rate_row * (position + 1.0))
    to_end[...] = jnp.exp(-rate_row * (tokens - 1.0 - position)).T

    pump(0, 1, 2)
    pump(1, 1, 2)
    gather_end(0, hbuf)
    normalize(hbuf, gain_a)
    for step in range(2, 4):
        pump(0, step, step + 1)
        pump(1, step, step + 1)
    pump(0, 4, depth)
    pump(1, 4, depth)
    start(2)
    finish(0)

    in_project(wa)

    def tail(b):
        return xin.at[pl.ds((b + 1) * tokens - taps, taps), :]

    halo_moves = (
        remote(tail(0), halos.at[0], halo_send.at[0], halo_recv.at[0], y_peer),
        remote(tail(1), halos.at[1], halo_send.at[1], halo_recv.at[1], y_peer),
        remote(
            tail(1),
            halos.at[2],
            halo_send.at[2],
            halo_recv.at[2],
            {"ctx": lax.rem(z + 2, depth) * 2 + 1 - y},
        ),
    )
    for move in halo_moves:
        move.start()
    pump(2, 1, 2)
    start(3)
    for move in halo_moves:
        move.wait()

    def medium_tile(q, carry):
        at = lanes(q)
        near0, near1, far = halos[0, :, at], halos[1, :, at], halos[2, :, at]
        far = jnp.where(z >= 2, far, jnp.zeros_like(far))
        befores = (jnp.where(y == 1, near0, far), jnp.where(y == 1, near1, near0))
        here, early = [], []
        for b in range(2):
            mine = [
                xin[b * tokens + k * taps : b * tokens + (k + 1) * taps, at] for k in range(blocks)
            ]
            here = here + mine
            early = early + [befores[b]] + mine[:-1]
        window = jnp.concatenate(
            [jnp.concatenate(early, axis=1), jnp.concatenate(here, axis=1)], axis=0
        )
        shape = (taps, 2 * blocks * LANES)
        group_of = lax.div(lax.rem(iota(shape, 1), LANES), per)
        total = jnp.zeros(shape, f32)
        for g in range(tile_groups):
            total = jnp.where(group_of == g, dot(toep_a[q * tile_groups + g], window), total)
        for k in range(2 * blocks):
            conv[k * taps : (k + 1) * taps, at] = total[:, k * LANES : (k + 1) * LANES]
        return carry

    lax.fori_loop(0, tiles, medium_tile, 0)
    product = proj[1] * conv[...]
    gated[...] = product.astype(bf16)
    finish(1)
    scatter_first(0, oa)
    give_back(0, product)
    scatter_second(0)
    pump(2, 2, 3)
    scatter_third(0)
    pump(3, 1, 2)
    scatter_end(0, hidden, abuf.at[lo, x, core])
    gather_first(1, abuf)
    pump(2, 3, depth)
    gather_second(1, abuf)
    pump(3, 2, 3)
    gather_third(1, abuf)
    gather_end(1, abuf)
    normalize(abuf, gain_b)
    finish(2)

    in_project(wb)

    def same_group(shape):
        return lax.div(iota(shape, 0), modes) == lax.div(iota(shape, 1), per)

    side = tile_groups * modes
    mine = pair * 2 + y
    for b in range(2):
        for q in range(tiles):
            at = slice(q * LANES, (q + 1) * LANES)
            values = xin[b * tokens : (b + 1) * tokens, at].astype(f32)
            ends = dot(to_end[q * side : (q + 1) * side, :], values, highest)
            ends = jnp.where(same_group((side, LANES)), ends, 0.0)
            total = ends[0:modes]
            for g in range(1, tile_groups):
                total = total + ends[g * modes : (g + 1) * modes]
            states[mine, b, :, at] = total

    def state_copy(off, index, to):
        return remote(
            states.at[index],
            states.at[index],
            state_send.at[off - 1],
            state_recv.at[off - 1],
            {"ctx": (lax.div(to, 2) * 2 + lo) * 2 + lax.rem(to, 2)},
        )

    def state_start(off, carry):
        state_copy(off, mine, lax.rem(mine + off, depth)).start()
        return carry

    lax.fori_loop(1, depth, state_start, 0)
    pump(3, 3, depth)

    def long_tile(q, carry):
        at = lanes(q)
        values = jnp.concatenate([xin[0:tokens, at], xin[tokens : 2 * tokens, at]], axis=1)
        group_of = lax.div(lax.rem(iota((tokens, 2 * LANES), 1), LANES), per)
        total = jnp.zeros((tokens, 2 * LANES), f32)
        for g in range(tile_groups):
            total = jnp.where(group_of == g, dot(toep_b[q * tile_groups + g], values), total)
        for b in range(2):
            conv[b * tokens : (b + 1) * tokens, at] = total[:, b * LANES : (b + 1) * LANES]
        return carry

    lax.fori_loop(0, tiles, long_tile, 0)

    def state_wait(off, carry):
        state_copy(off, lax.rem(mine - off + depth, depth), lax.rem(mine + off, depth)).wait_recv()
        return carry

    lax.fori_loop(1, depth, state_wait, 0)
    rates = rate_mc[:, pl.ds(pl.multiple_of(lo * channels, channels), channels)]

    def state_add(index, totals):
        result = []
        for b in range(2):
            block = 4 * pair + 2 * b + y
            total = totals[b]
            for k in range(2):
                j = 4 * lax.div(index, 2) + 2 * k + lax.rem(index, 2)
                gap = jnp.maximum(block - 1 - j, 0).astype(f32) * tokens
                term = jnp.exp(-rates * gap) * states[index, k]
                total = total + jnp.where(j < block, term, jnp.zeros_like(term))
            result.append(total)
        return tuple(result)

    zero = jnp.zeros((modes, channels), f32)
    entering = lax.fori_loop(0, depth, state_add, (zero, zero))
    for b in range(2):
        for q in range(tiles):
            at = slice(q * LANES, (q + 1) * LANES)
            spread = jnp.concatenate([entering[b][:, at]] * tile_groups, axis=0)
            spread = jnp.where(same_group((side, LANES)), spread, 0.0)
            conv[b * tokens : (b + 1) * tokens, at] += dot(
                from_start[:, q * side : (q + 1) * side], spread, highest
            )
    product = proj[1] * conv[...]
    gated[...] = product.astype(bf16)
    finish(3)
    scatter_first(1, ob)
    give_back(1, product)
    scatter_second(1)
    scatter_third(1)
    scatter_end(1, abuf.at[lo, x, core], mixed)

    give_end(0)
    give_end(1)
    gated_a_out[...] = turned_out[0]
    gated_b_out[...] = turned_out[1]

    def state_sent(off, carry):
        state_copy(off, mine, lax.rem(mine + off, depth)).wait_send()
        return carry

    lax.fori_loop(1, depth, state_sent, 0)
    for stream in range(4):
        all_sent(stream)


def per_device(
    n,
    ntp,
    hidden,
    norm_gain_a,
    in_weight_a,
    mr_filter,
    out_weight_a,
    norm_gain_b,
    in_weight_b,
    li_rate,
    li_residue,
    out_weight_b,
):
    tokens, width = hidden.shape
    dn, channels = in_weight_a.shape[1:]
    on = out_weight_a.shape[1]
    features = width * ntp
    groups, taps = mr_filter.shape
    modes = li_rate.shape[1]
    half = channels // 2
    mode_rows = jnp.stack([li_rate.reshape(-1), li_residue.reshape(-1)])
    rate_mc = jnp.repeat(li_rate.T, channels // groups, axis=1)
    vmem = pl.BlockSpec(memory_space=pltpu.VMEM)
    anywhere = pl.BlockSpec(memory_space=pl.ANY)
    flops = 2 * tokens * features * channels * 8 + 2 * tokens * channels * (tokens + 2 * taps) * 8
    return pl.pallas_call(
        functools.partial(kernel, n, ntp),
        out_shape=(
            jax.ShapeDtypeStruct((tokens, width), bf16),
            jax.ShapeDtypeStruct((channels, tokens), bf16),
            jax.ShapeDtypeStruct((channels, tokens), bf16),
        ),
        in_specs=[vmem, vmem, anywhere, vmem, anywhere, vmem, anywhere, vmem, vmem, vmem, vmem, anywhere],
        out_specs=(vmem, vmem, vmem),
        scratch_shapes=[
            pltpu.VMEM((2, 3, features, half), bf16),
            pltpu.VMEM((2, n, half, on), bf16),
            pltpu.VMEM((2, 3, features, half), bf16),
            pltpu.VMEM((2, n, half, on), bf16),
            pltpu.VMEM((2, 2, 2, tokens, width), bf16),
            pltpu.VMEM((2, 2, 2, tokens, width), bf16),
            pltpu.VMEM((2 * tokens, features), bf16),
            pltpu.VMEM((3, 2 * tokens, half), f32),
            pltpu.VMEM((2 * tokens, half), bf16),
            pltpu.VMEM((3, taps, half), bf16),
            pltpu.VMEM((2 * tokens, half), f32),
            pltpu.VMEM((2 * tokens, half), bf16),
            pltpu.VMEM((2, 2, 2, tokens, width), bf16),
            pltpu.VMEM((2, 2, 2, tokens, width), bf16),
            pltpu.VMEM((2, 2, tokens, width), bf16),
            pltpu.VMEM((2, 2, 2, tokens // 2, width), bf16),
            pltpu.VMEM((2, 2, tokens // 2, width), bf16),
            pltpu.VMEM((2, 2, tokens // 2, width), bf16),
            pltpu.VMEM((2, half, tokens), bf16),
            pltpu.VMEM((2, channels, tokens), bf16),
            pltpu.VMEM((n // 2, 2, modes, half), f32),
            pltpu.VMEM((groups // 2, taps, 2 * taps), bf16),
            pltpu.VMEM((groups // 2, tokens, tokens), bf16),
            pltpu.VMEM((groups, taps), f32),
            pltpu.VMEM((groups, tokens), f32),
            pltpu.VMEM((groups // 2 * modes, tokens), f32),
            pltpu.VMEM((tokens, groups // 2 * modes), f32),
            pltpu.SemaphoreType.DMA((4, 2, 2, n // 2)),
            pltpu.SemaphoreType.DMA((4, 2, 2, n // 2)),
            pltpu.SemaphoreType.DMA((4, 2, n // 2)),
            pltpu.SemaphoreType.DMA((4, 2, n // 2)),
            pltpu.SemaphoreType.DMA((5, 5)),
            pltpu.SemaphoreType.DMA((5, 5)),
            pltpu.SemaphoreType.DMA((n // 2 - 1,)),
            pltpu.SemaphoreType.DMA((n // 2 - 1,)),
            pltpu.SemaphoreType.DMA((3,)),
            pltpu.SemaphoreType.DMA((3,)),
            pltpu.SemaphoreType.DMA((4,)),
        ],
        cost_estimate=pl.CostEstimate(flops=flops, bytes_accessed=32 * 1024 * 1024, transcendentals=0),
        compiler_params=pltpu.CompilerParams(
            collective_id=0, has_side_effects=True, vmem_limit_bytes=60 * 1024 * 1024
        ),
    )(
        hidden,
        norm_gain_a.reshape(1, -1),
        in_weight_a,
        mr_filter,
        out_weight_a,
        norm_gain_b.reshape(1, -1),
        in_weight_b,
        li_rate,
        li_residue,
        mode_rows,
        rate_mc,
        out_weight_b,
    )


def solution(mesh):
    in_specs = (
        P("ctx", "tp"),
        P(),
        P(None, "ctx", "tp"),
        P("tp", None),
        P("tp", "ctx"),
        P(),
        P(None, "ctx", "tp"),
        P("tp", None),
        P("tp", None),
        P("tp", "ctx"),
    )
    out_specs = (P("ctx", "tp"), P("tp", "ctx"), P("tp", "ctx"))
    return jax.shard_map(
        functools.partial(per_device, mesh.shape["ctx"], mesh.shape["tp"]),
        mesh=mesh,
        in_specs=in_specs,
        out_specs=out_specs,
        check_vma=False,
    )
```

```python
import functools

import jax
import jax.numpy as jnp
from jax import lax
from jax.experimental import pallas as pl
from jax.experimental.pallas import tpu as pltpu
from jax.sharding import PartitionSpec as P

LANES = 128
MESH = pl.DeviceIdType.MESH
f32 = jnp.float32
bf16 = jnp.bfloat16
highest = lax.Precision.HIGHEST


def dot(a, b, precision=None):
    return lax.dot_general(
        a, b, (((1,), (0,)), ((), ())), precision=precision, preferred_element_type=f32
    )


def iota(shape, dim):
    return lax.broadcasted_iota(jnp.int32, shape, dim)


def kernel(
    n,
    ntp,
    hidden,
    gain_a,
    win_a,
    mr_filter,
    wout_a,
    gain_b,
    win_b,
    rate,
    residue,
    wout_b,
    mixed,
    gated_a_out,
    gated_b_out,
    wa,
    oa,
    wb,
    ob,
    hbuf,
    abuf,
    normed,
    proj,
    xin,
    halos,
    conv,
    gated,
    part,
    from_core,
    core_sum,
    from_first,
    first_sum,
    from_last,
    turned,
    turned_out,
    states,
    toep_a,
    toep_b,
    rows_a,
    rows_b,
    to_end,
    from_start,
    rates_here,
    line_send,
    line_recv,
    cross_send,
    cross_recv,
    swap_send,
    swap_recv,
    state_send,
    state_recv,
    halo_send,
    halo_recv,
    local_sems,
):
    me = lax.axis_index("ctx")
    mytp = lax.axis_index("tp")
    tokens, width = hidden.shape
    all_channels = win_a.shape[2]
    channels = all_channels // 2
    dn = win_a.shape[1]
    on = wout_a.shape[1]
    features = width * ntp
    all_groups, taps = mr_filter.shape
    groups = all_groups // 2
    modes = rate.shape[1]
    per = channels // groups
    tile_groups = LANES // per
    tiles = channels // LANES
    blocks = tokens // taps
    depth = n // 2
    rows2 = tokens // 2

    z, y = lax.div(me, 2), lax.rem(me, 2)
    lo = lax.rem(z, 2)
    pair = lax.div(z, 2)
    x, core = lax.div(mytp, 2), lax.rem(mytp, 2)
    core_peer = {"tp": x * 2 + 1 - core}
    x_peer = {"tp": (1 - x) * 2 + core}
    z_peer = {"ctx": (z + 1 - 2 * lo) * 2 + y}
    y_peer = {"ctx": z * 2 + 1 - y}

    barrier = pltpu.get_barrier_semaphore()

    def greet_ctx(off, carry):
        pl.semaphore_signal(
            barrier, inc=1, device_id={"ctx": lax.rem(me + off, n)}, device_id_type=MESH
        )
        return carry

    lax.fori_loop(1, n, greet_ctx, 0)
    for peer in (core_peer, x_peer):
        pl.semaphore_signal(barrier, inc=1, device_id=peer, device_id_type=MESH)

    def remote(src, dst, send, recv, peer):
        return pltpu.make_async_remote_copy(
            src_ref=src,
            dst_ref=dst,
            send_sem=send,
            recv_sem=recv,
            device_id=peer,
            device_id_type=MESH,
        )

    streams = ((win_a, wa), (wout_a, oa), (win_b, wb), (wout_b, ob))

    def slot(stream, owner):
        buffer = streams[stream][1]
        if stream in (0, 2):
            return buffer.at[:, pl.ds(pl.multiple_of(owner * dn, dn), dn), :]
        return buffer.at[owner]

    def own(stream, h):
        source = streams[stream][0]
        at = pl.ds(pl.multiple_of(h * channels, channels), channels)
        return source.at[:, :, at] if stream in (0, 2) else source.at[at, :]

    def along(way):
        return (z, 1) if way == 0 else (depth - 1 - z, -1)

    def line_copy(stream, way, step):
        zz, d = along(way)
        return remote(
            own(stream, lax.rem(z + step, 2)),
            slot(stream, me),
            line_send.at[stream, way, step],
            line_recv.at[stream, way, step],
            {"ctx": (z + d * step) * 2 + y},
        )

    def line_arrival(stream, way, step):
        zz, d = along(way)
        here = slot(stream, (z - d * step) * 2 + y)
        return remote(
            here,
            here,
            line_send.at[stream, way, step],
            line_recv.at[stream, way, step],
            {"ctx": (z - d * step) * 2 + y},
        )

    def cross_copy(stream, way, step, side):
        zz, d = along(way)
        here = slot(stream, (z - d * step) * 2 + side)
        return remote(
            here, here, cross_send.at[stream, way, step], cross_recv.at[stream, way, step], y_peer
        )

    def cross_own(stream):
        return remote(
            own(stream, lo),
            slot(stream, me),
            cross_send.at[stream, 0, 0],
            cross_recv.at[stream, 0, 0],
            y_peer,
        )

    def start(stream):
        cross_own(stream).start()

        def body(step, carry):
            for way in (0, 1):
                zz, d = along(way)

                @pl.when(zz + step < depth)
                def ahead():
                    line_copy(stream, way, step).start()

            return carry

        lax.fori_loop(1, depth, body, 0)

    def pump(stream, low, high):
        def body(step, carry):
            for way in (0, 1):
                zz, d = along(way)

                @pl.when(zz - step >= 0)
                def arrived():
                    line_arrival(stream, way, step).wait_recv()
                    cross_copy(stream, way, step, y).start()

            return carry

        if high > low:
            lax.fori_loop(low, high, body, 0)

    def finish(stream):
        cross_copy(stream, 0, 0, 1 - y).wait_recv()

        def body(step, carry):
            for way in (0, 1):
                zz, d = along(way)

                @pl.when(zz - step >= 0)
                def arrived():
                    cross_copy(stream, way, step, 1 - y).wait_recv()

            return carry

        lax.fori_loop(1, depth, body, 0)
        own_copy(stream).wait()

    def all_sent(stream):
        cross_own(stream).wait_send()

        def body(step, carry):
            for way in (0, 1):
                zz, d = along(way)

                @pl.when(zz + step < depth)
                def ahead():
                    line_copy(stream, way, step).wait_send()

                @pl.when(zz - step >= 0)
                def crossed():
                    cross_copy(stream, way, step, y).wait_send()

            return carry

        lax.fori_loop(1, depth, body, 0)

    def own_copy(stream):
        return pltpu.make_async_copy(own(stream, lo), slot(stream, me), local_sems.at[stream])

    upper, lower = pl.ds(0, rows2), pl.ds(rows2, rows2)

    def swap(use, step, src, dst, peer):
        return remote(src, dst, swap_send.at[use, step], swap_recv.at[use, step], peer)

    def gather_moves(use, buffer):
        def move(step, ref_out, ref_in, peer):
            return (swap(use, step, ref_out, ref_out, peer), swap(use, step, ref_in, ref_in, peer))

        return (
            move(0, buffer.at[lo, x, core, upper], buffer.at[1 - lo, x, core, upper], z_peer),
            move(1, buffer.at[lo, x, core, lower], buffer.at[lo, 1 - x, core, lower], x_peer),
            move(2, buffer.at[:, x, core, upper], buffer.at[:, 1 - x, core, upper], x_peer),
            move(3, buffer.at[lo, :, core, lower], buffer.at[1 - lo, :, core, lower], z_peer),
            move(4, buffer.at[:, :, core], buffer.at[:, :, 1 - core], core_peer),
        )

    def gather_first(use, buffer):
        moves = gather_moves(use, buffer)
        moves[0][0].start()
        moves[1][0].start()

    def gather_second(use, buffer):
        moves = gather_moves(use, buffer)
        moves[0][1].wait_recv()
        moves[2][0].start()
        moves[1][1].wait_recv()
        moves[3][0].start()

    def gather_third(use, buffer):
        moves = gather_moves(use, buffer)
        moves[2][1].wait_recv()
        moves[3][1].wait_recv()
        moves[4][0].start()

    def gather_end(use, buffer):
        moves = gather_moves(use, buffer)
        moves[4][1].wait_recv()
        for out, into in moves:
            out.wait_send()

    def normalize(buffer, gain):
        for b in range(2):
            total = jnp.zeros((tokens, 1), f32)
            for block in range(ntp):
                wide = buffer[b, block // 2, block % 2].astype(f32)
                total = total + jnp.sum(wide * wide, axis=1, keepdims=True)
            factor = lax.rsqrt(total / features + 1e-06)
            for block in range(ntp):
                at = slice(block * width, (block + 1) * width)
                wide = buffer[b, block // 2, block % 2].astype(f32)
                normed[b * tokens : (b + 1) * tokens, at] = (wide * factor * gain[:, at]).astype(bf16)

    def in_project(weight):
        def body(k, carry):
            proj[k] = dot(normed[...], weight[k])
            return carry

        lax.fori_loop(0, 3, body, 0)
        xin[...] = (proj[0] * proj[2]).astype(bf16)

    def out_blocks(buffer, c):
        def body(xx, carry):
            for j in range(width // on):
                block = dot(gated[...], buffer[(xx * 2 + c) * (width // on) + j]).astype(bf16)
                for b in range(2):
                    part[b, xx, c, :, j * on : (j + 1) * on] = block[b * tokens : (b + 1) * tokens]
            return carry

        lax.fori_loop(0, 2, body, 0)

    def scatter_moves(which):
        use = 2 + which
        return (
            swap(use, 0, part.at[:, :, 1 - core], from_core.at[which], core_peer),
            swap(use, 1, core_sum.at[1 - lo, :, upper], from_first.at[which, 0], z_peer),
            swap(use, 2, core_sum.at[:, 1 - x, lower], from_first.at[which, 1], x_peer),
            swap(use, 3, first_sum.at[0, 1 - x], from_last.at[which, 0], x_peer),
            swap(use, 4, first_sum.at[1, 1 - lo], from_last.at[which, 1], z_peer),
        )

    def scatter_first(which, buffer):
        moves = scatter_moves(which)
        out_blocks(buffer, 1 - core)
        moves[0].start()
        out_blocks(buffer, core)

    def scatter_second(which):
        moves = scatter_moves(which)
        moves[0].wait_recv()

        def add(b, xx, at):
            core_sum[b, xx, at] = (
                part[b, xx, core, at].astype(f32) + from_core[which, b, xx, at].astype(f32)
            ).astype(bf16)

        for xx in range(2):
            add(1 - lo, xx, upper)
        moves[1].start()
        for b in range(2):
            add(b, 1 - x, lower)
        moves[2].start()
        for xx in range(2):
            add(lo, xx, upper)
        for b in range(2):
            add(b, x, lower)

    def scatter_third(which):
        moves = scatter_moves(which)
        moves[1].wait_recv()
        for xx in range(2):
            first_sum[0, xx] = (
                core_sum[lo, xx, upper].astype(f32) + from_first[which, 0, xx].astype(f32)
            ).astype(bf16)
        moves[3].start()
        moves[2].wait_recv()
        for b in range(2):
            first_sum[1, b] = (
                core_sum[b, x, lower].astype(f32) + from_first[which, 1, b].astype(f32)
            ).astype(bf16)
        moves[4].start()

    def scatter_end(which, base, out):
        moves = scatter_moves(which)
        moves[3].wait_recv()
        out[upper] = (
            base[upper].astype(f32) + first_sum[0, x].astype(f32) + from_last[which, 0].astype(f32)
        ).astype(bf16)
        moves[4].wait_recv()
        out[lower] = (
            base[lower].astype(f32) + first_sum[1, lo].astype(f32) + from_last[which, 1].astype(f32)
        ).astype(bf16)
        for move in moves:
            move.wait_send()

    def give_move(which):
        return swap(
            4, which, turned.at[which], turned_out.at[which, pl.ds(pl.multiple_of(lo * channels, channels), channels)], z_peer
        )

    def give_back(which, product):
        flat = product.T.astype(bf16)
        at = pl.ds(pl.multiple_of(lo * channels, channels), channels)
        own_block = jnp.where(lo == 0, flat[:, :tokens], flat[:, tokens:])
        other = jnp.where(lo == 0, flat[:, tokens:], flat[:, :tokens])
        turned[which] = other
        turned_out[which, at] = own_block
        give_move(which).start()

    def give_end(which):
        give_move(which).wait_send()
        arriving = turned_out.at[which, pl.ds(pl.multiple_of((1 - lo) * channels, channels), channels)]
        swap(4, which, turned.at[which], arriving, z_peer).wait_recv()

    def lanes(q):
        return pl.ds(pl.multiple_of(q * LANES, LANES), LANES)

    hbuf[lo, x, core] = hidden[...]
    for stream in range(4):
        own_copy(stream).start()
    pl.semaphore_wait(barrier, (n - 1) + 2)

    gather_first(0, hbuf)
    start(0)
    start(1)

    flip = (lax.rem(iota((taps, taps), 0) + iota((taps, taps), 1), taps) == 0).astype(bf16)
    rows_a[...] = dot(mr_filter[...], flip)
    lag = lax.rem(tokens - iota((all_groups, tokens), 1), tokens).astype(f32)
    impulse = jnp.zeros((all_groups, tokens), f32)
    for m in range(modes):
        r = rate[:, m : m + 1]
        impulse = impulse + residue[:, m : m + 1] * jnp.sqrt(2.0 * r) * jnp.exp(-r * lag)
    rows_b[...] = impulse

    def build_a(g, carry):
        row = jnp.broadcast_to(rows_a[pl.ds(lo * groups + g, 1), :], (taps, taps))
        rolled = pltpu.roll(row, 0, 1, stride=1, stride_axis=0)
        below = iota((taps, taps), 1) <= iota((taps, taps), 0)
        toep_a[g, :, :taps] = jnp.where(below, 0.0, rolled).astype(bf16)
        toep_a[g, :, taps:] = jnp.where(below, rolled, 0.0).astype(bf16)
        return carry

    def build_b(g, carry):
        row = jnp.broadcast_to(rows_b[pl.ds(lo * groups + g, 1), :], (tokens, tokens))
        rolled = pltpu.roll(row, 0, 1, stride=1, stride_axis=0)
        below = iota((tokens, tokens), 1) <= iota((tokens, tokens), 0)
        toep_b[g] = jnp.where(below, rolled, 0.0).astype(bf16)
        return carry

    lax.fori_loop(0, groups, build_a, 0)
    gather_second(0, hbuf)
    lax.fori_loop(0, groups, build_b, 0)
    gather_third(0, hbuf)

    def mode_row(ref):
        here = ref[pl.ds(pl.multiple_of(lo * groups, 8), groups), :]
        shape = (modes, groups * modes)
        pick = (iota(shape, 0) == lax.rem(iota(shape, 1), modes)).astype(f32)
        spread = dot(here, pick, highest)
        keep = iota(spread.shape, 0) == lax.div(iota(spread.shape, 1), modes)
        return jnp.sum(jnp.where(keep, spread, 0.0), axis=0, keepdims=True)

    rate_row = mode_row(rate)
    weight_row = mode_row(residue) * jnp.sqrt(2.0 * rate_row)
    shape = (modes, groups * modes)
    by_mode = jnp.where(iota(shape, 0) == lax.rem(iota(shape, 1), modes), rate_row, 0.0)
    shape = (groups * modes, channels)
    pick = (lax.div(iota(shape, 0), modes) == lax.div(iota(shape, 1), per)).astype(f32)
    rates_here[...] = dot(by_mode, pick, highest)
    position = iota((tokens, groups * modes), 0).astype(f32)
    from_start[...] = weight_row * jnp.exp(-rate_row * (position + 1.0))
    to_end[...] = jnp.exp(-rate_row * (tokens - 1.0 - position)).T

    pump(0, 1, 2)
    pump(1, 1, 2)
    gather_end(0, hbuf)
    normalize(hbuf, gain_a)
    pump(0, 2, 3)
    pump(1, 2, 3)
    pump(0, 3, depth)
    start(2)
    pump(1, 3, depth)
    finish(0)

    in_project(wa)

    def tail(b):
        return xin.at[pl.ds((b + 1) * tokens - taps, taps), :]

    halo_moves = (
        remote(tail(0), halos.at[0], halo_send.at[0], halo_recv.at[0], y_peer),
        remote(tail(1), halos.at[1], halo_send.at[1], halo_recv.at[1], y_peer),
        remote(
            tail(1),
            halos.at[2],
            halo_send.at[2],
            halo_recv.at[2],
            {"ctx": lax.rem(z + 2, depth) * 2 + 1 - y},
        ),
    )
    for move in halo_moves:
        move.start()
    for move in halo_moves:
        move.wait()

    def medium_tile(q, carry):
        at = lanes(q)
        near0, near1, far = halos[0, :, at], halos[1, :, at], halos[2, :, at]
        far = jnp.where(z >= 2, far, jnp.zeros_like(far))
        befores = (jnp.where(y == 1, near0, far), jnp.where(y == 1, near1, near0))
        here, early = [], []
        for b in range(2):
            mine = [
                xin[b * tokens + k * taps : b * tokens + (k + 1) * taps, at] for k in range(blocks)
            ]
            here = here + mine
            early = early + [befores[b]] + mine[:-1]
        window = jnp.concatenate(
            [jnp.concatenate(early, axis=1), jnp.concatenate(here, axis=1)], axis=0
        )
        shape = (taps, 2 * blocks * LANES)
        group_of = lax.div(lax.rem(iota(shape, 1), LANES), per)
        total = jnp.zeros(shape, f32)
        for g in range(tile_groups):
            total = jnp.where(group_of == g, dot(toep_a[q * tile_groups + g], window), total)
        for k in range(2 * blocks):
            conv[k * taps : (k + 1) * taps, at] = total[:, k * LANES : (k + 1) * LANES]
        return carry

    lax.fori_loop(0, tiles, medium_tile, 0)
    product = proj[1] * conv[...]
    gated[...] = product.astype(bf16)
    finish(1)
    scatter_first(0, oa)
    give_back(0, product)
    pump(2, 1, 2)
    start(3)
    scatter_second(0)
    scatter_third(0)
    pump(2, 2, 3)
    scatter_end(0, hidden, abuf.at[lo, x, core])
    gather_first(1, abuf)
    gather_second(1, abuf)
    pump(2, 3, depth)
    gather_third(1, abuf)
    pump(3, 1, 2)
    gather_end(1, abuf)
    normalize(abuf, gain_b)
    finish(2)

    pump(3, 2, 3)
    in_project(wb)

    def same_group(shape):
        return lax.div(iota(shape, 0), modes) == lax.div(iota(shape, 1), per)

    side = tile_groups * modes
    mine = pair * 2 + y
    for b in range(2):
        for q in range(tiles):
            at = slice(q * LANES, (q + 1) * LANES)
            values = xin[b * tokens : (b + 1) * tokens, at].astype(f32)
            ends = dot(to_end[q * side : (q + 1) * side, :], values, highest)
            ends = jnp.where(same_group((side, LANES)), ends, 0.0)
            total = ends[0:modes]
            for g in range(1, tile_groups):
                total = total + ends[g * modes : (g + 1) * modes]
            states[mine, b, :, at] = total

    def state_copy(off, index, to):
        return remote(
            states.at[index],
            states.at[index],
            state_send.at[off - 1],
            state_recv.at[off - 1],
            {"ctx": (lax.div(to, 2) * 2 + lo) * 2 + lax.rem(to, 2)},
        )

    def state_start(off, carry):
        state_copy(off, mine, lax.rem(mine + off, depth)).start()
        return carry

    lax.fori_loop(1, depth, state_start, 0)
    pump(3, 3, depth)

    def long_tile(q, carry):
        at = lanes(q)
        values = jnp.concatenate([xin[0:tokens, at], xin[tokens : 2 * tokens, at]], axis=1)
        group_of = lax.div(lax.rem(iota((tokens, 2 * LANES), 1), LANES), per)
        total = jnp.zeros((tokens, 2 * LANES), f32)
        for g in range(tile_groups):
            total = jnp.where(group_of == g, dot(toep_b[q * tile_groups + g], values), total)
        for b in range(2):
            conv[b * tokens : (b + 1) * tokens, at] = total[:, b * LANES : (b + 1) * LANES]
        return carry

    lax.fori_loop(0, tiles, long_tile, 0)

    def state_wait(off, carry):
        state_copy(off, lax.rem(mine - off + depth, depth), lax.rem(mine + off, depth)).wait_recv()
        return carry

    lax.fori_loop(1, depth, state_wait, 0)
    rates = rates_here[...]

    def state_add(index, totals):
        result = []
        for b in range(2):
            block = 4 * pair + 2 * b + y
            total = totals[b]
            for k in range(2):
                j = 4 * lax.div(index, 2) + 2 * k + lax.rem(index, 2)
                gap = jnp.maximum(block - 1 - j, 0).astype(f32) * tokens
                term = jnp.exp(-rates * gap) * states[index, k]
                total = total + jnp.where(j < block, term, jnp.zeros_like(term))
            result.append(total)
        return tuple(result)

    zero = jnp.zeros((modes, channels), f32)
    entering = lax.fori_loop(0, depth, state_add, (zero, zero))
    for b in range(2):
        for q in range(tiles):
            at = slice(q * LANES, (q + 1) * LANES)
            spread = jnp.concatenate([entering[b][:, at]] * tile_groups, axis=0)
            spread = jnp.where(same_group((side, LANES)), spread, 0.0)
            conv[b * tokens : (b + 1) * tokens, at] += dot(
                from_start[:, q * side : (q + 1) * side], spread, highest
            )
    product = proj[1] * conv[...]
    gated[...] = product.astype(bf16)
    finish(3)
    scatter_first(1, ob)
    give_back(1, product)
    scatter_second(1)
    scatter_third(1)
    scatter_end(1, abuf.at[lo, x, core], mixed)

    give_end(0)
    give_end(1)
    gated_a_out[...] = turned_out[0]
    gated_b_out[...] = turned_out[1]

    def state_sent(off, carry):
        state_copy(off, mine, lax.rem(mine + off, depth)).wait_send()
        return carry

    lax.fori_loop(1, depth, state_sent, 0)
    for stream in range(4):
        all_sent(stream)


def per_device(
    n,
    ntp,
    hidden,
    norm_gain_a,
    in_weight_a,
    mr_filter,
    out_weight_a,
    norm_gain_b,
    in_weight_b,
    li_rate,
    li_residue,
    out_weight_b,
):
    tokens, width = hidden.shape
    dn, channels = in_weight_a.shape[1:]
    on = out_weight_a.shape[1]
    features = width * ntp
    groups, taps = mr_filter.shape
    modes = li_rate.shape[1]
    half = channels // 2
    vmem = pl.BlockSpec(memory_space=pltpu.VMEM)
    anywhere = pl.BlockSpec(memory_space=pl.ANY)
    flops = 2 * tokens * features * channels * 8 + 2 * tokens * channels * (tokens + 2 * taps) * 8
    return pl.pallas_call(
        functools.partial(kernel, n, ntp),
        out_shape=(
            jax.ShapeDtypeStruct((tokens, width), bf16),
            jax.ShapeDtypeStruct((channels, tokens), bf16),
            jax.ShapeDtypeStruct((channels, tokens), bf16),
        ),
        in_specs=[vmem, vmem, anywhere, vmem, anywhere, vmem, anywhere, vmem, vmem, anywhere],
        out_specs=(vmem, vmem, vmem),
        scratch_shapes=[
            pltpu.VMEM((3, features, half), bf16),
            pltpu.VMEM((n, half, on), bf16),
            pltpu.VMEM((3, features, half), bf16),
            pltpu.VMEM((n, half, on), bf16),
            pltpu.VMEM((2, 2, 2, tokens, width), bf16),
            pltpu.VMEM((2, 2, 2, tokens, width), bf16),
            pltpu.VMEM((2 * tokens, features), bf16),
            pltpu.VMEM((3, 2 * tokens, half), f32),
            pltpu.VMEM((2 * tokens, half), bf16),
            pltpu.VMEM((3, taps, half), bf16),
            pltpu.VMEM((2 * tokens, half), f32),
            pltpu.VMEM((2 * tokens, half), bf16),
            pltpu.VMEM((2, 2, 2, tokens, width), bf16),
            pltpu.VMEM((2, 2, 2, tokens, width), bf16),
            pltpu.VMEM((2, 2, tokens, width), bf16),
            pltpu.VMEM((2, 2, 2, tokens // 2, width), bf16),
            pltpu.VMEM((2, 2, tokens // 2, width), bf16),
            pltpu.VMEM((2, 2, tokens // 2, width), bf16),
            pltpu.VMEM((2, half, tokens), bf16),
            pltpu.VMEM((2, channels, tokens), bf16),
            pltpu.VMEM((n // 2, 2, modes, half), f32),
            pltpu.VMEM((groups // 2, taps, 2 * taps), bf16),
            pltpu.VMEM((groups // 2, tokens, tokens), bf16),
            pltpu.VMEM((groups, taps), f32),
            pltpu.VMEM((groups, tokens), f32),
            pltpu.VMEM((groups // 2 * modes, tokens), f32),
            pltpu.VMEM((tokens, groups // 2 * modes), f32),
            pltpu.VMEM((modes, half), f32),
            pltpu.SemaphoreType.DMA((4, 2, n // 2)),
            pltpu.SemaphoreType.DMA((4, 2, n // 2)),
            pltpu.SemaphoreType.DMA((4, 2, n // 2)),
            pltpu.SemaphoreType.DMA((4, 2, n // 2)),
            pltpu.SemaphoreType.DMA((5, 5)),
            pltpu.SemaphoreType.DMA((5, 5)),
            pltpu.SemaphoreType.DMA((n // 2 - 1,)),
            pltpu.SemaphoreType.DMA((n // 2 - 1,)),
            pltpu.SemaphoreType.DMA((3,)),
            pltpu.SemaphoreType.DMA((3,)),
            pltpu.SemaphoreType.DMA((4,)),
        ],
        cost_estimate=pl.CostEstimate(flops=flops, bytes_accessed=32 * 1024 * 1024, transcendentals=0),
        compiler_params=pltpu.CompilerParams(
            collective_id=0, has_side_effects=True, vmem_limit_bytes=60 * 1024 * 1024
        ),
    )(
        hidden,
        norm_gain_a.reshape(1, -1),
        in_weight_a,
        mr_filter,
        out_weight_a,
        norm_gain_b.reshape(1, -1),
        in_weight_b,
        li_rate,
        li_residue,
        out_weight_b,
    )


def solution(mesh):
    in_specs = (
        P("ctx", "tp"),
        P(),
        P(None, "ctx", "tp"),
        P("tp", None),
        P("tp", "ctx"),
        P(),
        P(None, "ctx", "tp"),
        P("tp", None),
        P("tp", None),
        P("tp", "ctx"),
    )
    out_specs = (P("ctx", "tp"), P("tp", "ctx"), P("tp", "ctx"))
    return jax.shard_map(
        functools.partial(per_device, mesh.shape["ctx"], mesh.shape["tp"]),
        mesh=mesh,
        in_specs=in_specs,
        out_specs=out_specs,
        check_vma=False,
    )
```

```python
import functools

import jax
import jax.numpy as jnp
from jax import lax
from jax.experimental import pallas as pl
from jax.experimental.pallas import tpu as pltpu
from jax.sharding import PartitionSpec as P

LANES = 128
MESH = pl.DeviceIdType.MESH
f32 = jnp.float32
bf16 = jnp.bfloat16
highest = lax.Precision.HIGHEST


def dot(a, b, precision=None):
    return lax.dot_general(
        a, b, (((1,), (0,)), ((), ())), precision=precision, preferred_element_type=f32
    )


def iota(shape, dim):
    return lax.broadcasted_iota(jnp.int32, shape, dim)


def kernel(
    n,
    ntp,
    hidden,
    gain_a,
    win_a,
    mr_filter,
    wout_a,
    gain_b,
    win_b,
    rate,
    residue,
    wout_b,
    mixed,
    gated_a_out,
    gated_b_out,
    wa,
    oa,
    wb,
    ob,
    hbuf,
    abuf,
    normed,
    proj,
    xin,
    halos,
    conv,
    gated,
    part,
    from_core,
    core_sum,
    from_first,
    first_sum,
    from_last,
    turned,
    turned_out,
    states,
    toep_a,
    toep_b,
    rows_a,
    rows_b,
    to_end,
    from_start,
    rates_here,
    line_send,
    line_recv,
    cross_send,
    cross_recv,
    swap_send,
    swap_recv,
    state_send,
    state_recv,
    halo_send,
    halo_recv,
    local_sems,
):
    me = lax.axis_index("ctx")
    mytp = lax.axis_index("tp")
    tokens, width = hidden.shape
    all_channels = win_a.shape[2]
    channels = all_channels // 2
    dn = win_a.shape[1]
    on = wout_a.shape[1]
    features = width * ntp
    all_groups, taps = mr_filter.shape
    groups = all_groups // 2
    modes = rate.shape[1]
    per = channels // groups
    tile_groups = LANES // per
    tiles = channels // LANES
    blocks = tokens // taps
    depth = n // 2
    rows2 = tokens // 2

    z, y = lax.div(me, 2), lax.rem(me, 2)
    lo = lax.rem(z, 2)
    pair = lax.div(z, 2)
    x, core = lax.div(mytp, 2), lax.rem(mytp, 2)
    core_peer = {"tp": x * 2 + 1 - core}
    x_peer = {"tp": (1 - x) * 2 + core}
    z_peer = {"ctx": (z + 1 - 2 * lo) * 2 + y}
    y_peer = {"ctx": z * 2 + 1 - y}

    barrier = pltpu.get_barrier_semaphore()

    def greet_ctx(off, carry):
        pl.semaphore_signal(
            barrier, inc=1, device_id={"ctx": lax.rem(me + off, n)}, device_id_type=MESH
        )
        return carry

    lax.fori_loop(1, n, greet_ctx, 0)
    for peer in (core_peer, x_peer):
        pl.semaphore_signal(barrier, inc=1, device_id=peer, device_id_type=MESH)

    def remote(src, dst, send, recv, peer):
        return pltpu.make_async_remote_copy(
            src_ref=src,
            dst_ref=dst,
            send_sem=send,
            recv_sem=recv,
            device_id=peer,
            device_id_type=MESH,
        )

    def buffers(stream):
        return ((win_a, wa, wout_a, oa), (win_b, wb, wout_b, ob))[stream // 4]

    def slot(stream, h, owner):
        if stream % 4 < 3:
            rows = pl.ds(pl.multiple_of(owner * dn, dn), dn)
            return buffers(stream)[1].at[h, stream % 4, rows, :]
        return buffers(stream)[3].at[h, owner]

    def own(stream, h):
        at = pl.ds(pl.multiple_of(h * channels, channels), channels)
        if stream % 4 < 3:
            return buffers(stream)[0].at[stream % 4, :, at]
        return buffers(stream)[2].at[at, :]

    def along(way):
        return (z, 1) if way == 0 else (depth - 1 - z, -1)

    def line_copy(stream, way, kind, step, first=False):
        zz, d = along(way)
        h = 1 - lo if kind == 0 else lo
        owner = (z - d * step) * 2 + y
        return remote(
            own(stream, h) if first else slot(stream, h, owner),
            slot(stream, h, owner),
            line_send.at[stream, way, kind, step],
            line_recv.at[stream, way, kind, step],
            {"ctx": (z + d) * 2 + y},
        )

    def line_arrival(stream, way, kind, step):
        zz, d = along(way)
        h = lo if kind == 0 else 1 - lo
        here = slot(stream, h, (z - d * (step + 1)) * 2 + y)
        return remote(
            here,
            here,
            line_send.at[stream, way, kind, step],
            line_recv.at[stream, way, kind, step],
            {"ctx": (z - d) * 2 + y},
        )

    def cross_copy(stream, way, step, side):
        zz, d = along(way)
        here = slot(stream, lo, (z - d * step) * 2 + side)
        return remote(
            here, here, cross_send.at[stream, way, step], cross_recv.at[stream, way, step], y_peer
        )

    def cross_own(stream):
        return remote(
            own(stream, lo),
            slot(stream, lo, me),
            cross_send.at[stream, 0, 0],
            cross_recv.at[stream, 0, 0],
            y_peer,
        )

    def start(stream):
        for kind in (1, 0):
            for way in (0, 1):
                zz, d = along(way)

                @pl.when(zz + 1 + kind < depth)
                def ahead():
                    line_copy(stream, way, kind, 0, True).start()

        cross_own(stream).start()

    def pump(stream, low, high):
        def body(step, carry):
            for way in (0, 1):
                zz, d = along(way)

                @pl.when(zz - step >= 0)
                def arrived():
                    line_arrival(stream, way, 0, step - 1).wait_recv()

                    @pl.when(zz + 2 < depth)
                    def through():
                        line_copy(stream, way, 1, step).start()

                    cross_copy(stream, way, step, y).start()

                    @pl.when(zz + 1 < depth)
                    def near():
                        line_arrival(stream, way, 1, step - 1).wait_recv()
                        line_copy(stream, way, 0, step).start()

            return carry

        if min(high, depth) > low:
            lax.fori_loop(low, min(high, depth), body, 0)

    def finish(stream):
        cross_copy(stream, 0, 0, 1 - y).wait_recv()

        def body(step, carry):
            for way in (0, 1):
                zz, d = along(way)

                @pl.when(zz - step >= 0)
                def arrived():
                    cross_copy(stream, way, step, 1 - y).wait_recv()

            return carry

        lax.fori_loop(1, depth, body, 0)
        own_copy(stream).wait()

    def all_sent(stream):
        cross_own(stream).wait_send()

        def body(step, carry):
            for way in (0, 1):
                zz, d = along(way)

                @pl.when(zz - step >= 0)
                def passed():
                    @pl.when(zz + 1 < depth)
                    def near():
                        line_copy(stream, way, 0, step).wait_send()

                    @pl.when(zz + 2 < depth)
                    def through():
                        line_copy(stream, way, 1, step).wait_send()

                    @pl.when(step > 0)
                    def crossed():
                        cross_copy(stream, way, step, y).wait_send()

            return carry

        lax.fori_loop(0, depth, body, 0)

    def own_copy(stream):
        return pltpu.make_async_copy(own(stream, lo), slot(stream, lo, me), local_sems.at[stream])

    upper, lower = pl.ds(0, rows2), pl.ds(rows2, rows2)

    def swap(use, step, src, dst, peer):
        return remote(src, dst, swap_send.at[use, step], swap_recv.at[use, step], peer)

    def gather_moves(use, buffer):
        def move(step, ref_out, ref_in, peer):
            return (swap(use, step, ref_out, ref_out, peer), swap(use, step, ref_in, ref_in, peer))

        return (
            move(0, buffer.at[lo, x, core, upper], buffer.at[1 - lo, x, core, upper], z_peer),
            move(1, buffer.at[lo, x, core, lower], buffer.at[lo, 1 - x, core, lower], x_peer),
            move(2, buffer.at[:, x, core, upper], buffer.at[:, 1 - x, core, upper], x_peer),
            move(3, buffer.at[lo, :, core, lower], buffer.at[1 - lo, :, core, lower], z_peer),
            move(4, buffer.at[:, :, core], buffer.at[:, :, 1 - core], core_peer),
        )

    def gather_first(use, buffer):
        moves = gather_moves(use, buffer)
        moves[0][0].start()
        moves[1][0].start()

    def gather_second(use, buffer):
        moves = gather_moves(use, buffer)
        moves[0][1].wait_recv()
        moves[2][0].start()
        moves[1][1].wait_recv()
        moves[3][0].start()

    def gather_third(use, buffer):
        moves = gather_moves(use, buffer)
        moves[2][1].wait_recv()
        moves[3][1].wait_recv()
        moves[4][0].start()

    def gather_end(use, buffer):
        moves = gather_moves(use, buffer)
        moves[4][1].wait_recv()
        for out, into in moves:
            out.wait_send()

    def normalize(buffer, gain):
        for b in range(2):
            total = jnp.zeros((tokens, 1), f32)
            for block in range(ntp):
                wide = buffer[b, block // 2, block % 2].astype(f32)
                total = total + jnp.sum(wide * wide, axis=1, keepdims=True)
            factor = lax.rsqrt(total / features + 1e-06)
            for block in range(ntp):
                at = slice(block * width, (block + 1) * width)
                wide = buffer[b, block // 2, block % 2].astype(f32)
                normed[b * tokens : (b + 1) * tokens, at] = (wide * factor * gain[:, at]).astype(bf16)

    def in_project(weight, k):
        proj[k] = dot(normed[...], weight[lo, k])

    def in_product():
        xin[...] = (proj[0] * proj[2]).astype(bf16)

    def out_blocks(buffer, c):
        def body(xx, carry):
            for j in range(width // on):
                block = dot(gated[...], buffer[lo, (xx * 2 + c) * (width // on) + j]).astype(bf16)
                for b in range(2):
                    part[b, xx, c, :, j * on : (j + 1) * on] = block[b * tokens : (b + 1) * tokens]
            return carry

        lax.fori_loop(0, 2, body, 0)

    def scatter_moves(which):
        use = 2 + which
        return (
            swap(use, 0, part.at[:, :, 1 - core], from_core.at[which], core_peer),
            swap(use, 1, core_sum.at[1 - lo, :, upper], from_first.at[which, 0], z_peer),
            swap(use, 2, core_sum.at[:, 1 - x, lower], from_first.at[which, 1], x_peer),
            swap(use, 3, first_sum.at[0, 1 - x], from_last.at[which, 0], x_peer),
            swap(use, 4, first_sum.at[1, 1 - lo], from_last.at[which, 1], z_peer),
        )

    def scatter_first(which, buffer):
        moves = scatter_moves(which)
        out_blocks(buffer, 1 - core)
        moves[0].start()
        out_blocks(buffer, core)

    def scatter_second(which):
        moves = scatter_moves(which)
        moves[0].wait_recv()

        def add(b, xx, at):
            core_sum[b, xx, at] = (
                part[b, xx, core, at].astype(f32) + from_core[which, b, xx, at].astype(f32)
            ).astype(bf16)

        for xx in range(2):
            add(1 - lo, xx, upper)
        moves[1].start()
        for b in range(2):
            add(b, 1 - x, lower)
        moves[2].start()
        for xx in range(2):
            add(lo, xx, upper)
        for b in range(2):
            add(b, x, lower)

    def scatter_third(which):
        moves = scatter_moves(which)
        moves[1].wait_recv()
        for xx in range(2):
            first_sum[0, xx] = (
                core_sum[lo, xx, upper].astype(f32) + from_first[which, 0, xx].astype(f32)
            ).astype(bf16)
        moves[3].start()
        moves[2].wait_recv()
        for b in range(2):
            first_sum[1, b] = (
                core_sum[b, x, lower].astype(f32) + from_first[which, 1, b].astype(f32)
            ).astype(bf16)
        moves[4].start()

    def scatter_end(which, base, out):
        moves = scatter_moves(which)
        moves[3].wait_recv()
        out[upper] = (
            base[upper].astype(f32) + first_sum[0, x].astype(f32) + from_last[which, 0].astype(f32)
        ).astype(bf16)
        moves[4].wait_recv()
        out[lower] = (
            base[lower].astype(f32) + first_sum[1, lo].astype(f32) + from_last[which, 1].astype(f32)
        ).astype(bf16)
        for move in moves:
            move.wait_send()

    def give_move(which):
        return swap(
            4, which, turned.at[which], turned_out.at[which, pl.ds(pl.multiple_of(lo * channels, channels), channels)], z_peer
        )

    def give_back(which, product):
        flat = product.T.astype(bf16)
        at = pl.ds(pl.multiple_of(lo * channels, channels), channels)
        own_block = jnp.where(lo == 0, flat[:, :tokens], flat[:, tokens:])
        other = jnp.where(lo == 0, flat[:, tokens:], flat[:, :tokens])
        turned[which] = other
        turned_out[which, at] = own_block
        give_move(which).start()

    def give_end(which):
        give_move(which).wait_send()
        arriving = turned_out.at[which, pl.ds(pl.multiple_of((1 - lo) * channels, channels), channels)]
        swap(4, which, turned.at[which], arriving, z_peer).wait_recv()

    def lanes(q):
        return pl.ds(pl.multiple_of(q * LANES, LANES), LANES)

    hbuf[lo, x, core] = hidden[...]
    for stream in range(8):
        own_copy(stream).start()
    pl.semaphore_wait(barrier, (n - 1) + 2)

    gather_first(0, hbuf)
    start(0)
    start(1)

    flip = (lax.rem(iota((taps, taps), 0) + iota((taps, taps), 1), taps) == 0).astype(bf16)
    rows_a[...] = dot(mr_filter[...], flip)
    lag = lax.rem(tokens - iota((all_groups, tokens), 1), tokens).astype(f32)
    impulse = jnp.zeros((all_groups, tokens), f32)
    for m in range(modes):
        r = rate[:, m : m + 1]
        impulse = impulse + residue[:, m : m + 1] * jnp.sqrt(2.0 * r) * jnp.exp(-r * lag)
    rows_b[...] = impulse

    def build_a(g, carry):
        row = jnp.broadcast_to(rows_a[pl.ds(lo * groups + g, 1), :], (taps, taps))
        rolled = pltpu.roll(row, 0, 1, stride=1, stride_axis=0)
        below = iota((taps, taps), 1) <= iota((taps, taps), 0)
        toep_a[g, :, :taps] = jnp.where(below, 0.0, rolled).astype(bf16)
        toep_a[g, :, taps:] = jnp.where(below, rolled, 0.0).astype(bf16)
        return carry

    def build_b(g, carry):
        row = jnp.broadcast_to(rows_b[pl.ds(lo * groups + g, 1), :], (tokens, tokens))
        rolled = pltpu.roll(row, 0, 1, stride=1, stride_axis=0)
        below = iota((tokens, tokens), 1) <= iota((tokens, tokens), 0)
        toep_b[g] = jnp.where(below, rolled, 0.0).astype(bf16)
        return carry

    lax.fori_loop(0, groups, build_a, 0)
    pump(0, 1, 2)
    start(2)
    gather_second(0, hbuf)
    lax.fori_loop(0, groups, build_b, 0)
    pump(0, 2, 3)
    pump(1, 1, 2)
    start(3)
    gather_third(0, hbuf)

    def mode_row(ref):
        here = ref[pl.ds(pl.multiple_of(lo * groups, 8), groups), :]
        shape = (modes, groups * modes)
        pick = (iota(shape, 0) == lax.rem(iota(shape, 1), modes)).astype(f32)
        spread = dot(here, pick, highest)
        keep = iota(spread.shape, 0) == lax.div(iota(spread.shape, 1), modes)
        return jnp.sum(jnp.where(keep, spread, 0.0), axis=0, keepdims=True)

    rate_row = mode_row(rate)
    weight_row = mode_row(residue) * jnp.sqrt(2.0 * rate_row)
    shape = (modes, groups * modes)
    by_mode = jnp.where(iota(shape, 0) == lax.rem(iota(shape, 1), modes), rate_row, 0.0)
    shape = (groups * modes, channels)
    pick = (lax.div(iota(shape, 0), modes) == lax.div(iota(shape, 1), per)).astype(f32)
    rates_here[...] = dot(by_mode, pick, highest)
    position = iota((tokens, groups * modes), 0).astype(f32)
    from_start[...] = weight_row * jnp.exp(-rate_row * (position + 1.0))
    to_end[...] = jnp.exp(-rate_row * (tokens - 1.0 - position)).T

    pump(0, 3, depth)
    pump(1, 2, 3)
    pump(2, 1, 2)
    start(4)
    gather_end(0, hbuf)
    normalize(hbuf, gain_a)
    pump(1, 3, depth)
    pump(2, 2, 3)
    finish(0)
    in_project(wa, 0)
    pump(3, 1, 2)
    start(5)
    finish(1)
    in_project(wa, 1)
    pump(2, 3, depth)
    finish(2)
    in_project(wa, 2)
    in_product()

    def tail(b):
        return xin.at[pl.ds((b + 1) * tokens - taps, taps), :]

    halo_moves = (
        remote(tail(0), halos.at[0], halo_send.at[0], halo_recv.at[0], y_peer),
        remote(tail(1), halos.at[1], halo_send.at[1], halo_recv.at[1], y_peer),
        remote(
            tail(1),
            halos.at[2],
            halo_send.at[2],
            halo_recv.at[2],
            {"ctx": lax.rem(z + 2, depth) * 2 + 1 - y},
        ),
    )
    for move in halo_moves:
        move.start()
    pump(3, 2, 3)
    pump(4, 1, 2)
    start(6)
    for move in halo_moves:
        move.wait()

    def medium_tile(q, carry):
        at = lanes(q)
        near0, near1, far = halos[0, :, at], halos[1, :, at], halos[2, :, at]
        far = jnp.where(z >= 2, far, jnp.zeros_like(far))
        befores = (jnp.where(y == 1, near0, far), jnp.where(y == 1, near1, near0))
        here, early = [], []
        for b in range(2):
            mine = [
                xin[b * tokens + k * taps : b * tokens + (k + 1) * taps, at] for k in range(blocks)
            ]
            here = here + mine
            early = early + [befores[b]] + mine[:-1]
        window = jnp.concatenate(
            [jnp.concatenate(early, axis=1), jnp.concatenate(here, axis=1)], axis=0
        )
        shape = (taps, 2 * blocks * LANES)
        group_of = lax.div(lax.rem(iota(shape, 1), LANES), per)
        total = jnp.zeros(shape, f32)
        for g in range(tile_groups):
            total = jnp.where(group_of == g, dot(toep_a[q * tile_groups + g], window), total)
        for k in range(2 * blocks):
            conv[k * taps : (k + 1) * taps, at] = total[:, k * LANES : (k + 1) * LANES]
        return carry

    lax.fori_loop(0, tiles, medium_tile, 0)
    product = proj[1] * conv[...]
    gated[...] = product.astype(bf16)
    pump(3, 3, depth)
    pump(4, 2, 3)
    pump(5, 1, 2)
    start(7)
    finish(3)
    scatter_first(0, oa)
    give_back(0, product)
    scatter_second(0)
    scatter_third(0)
    pump(4, 3, depth)
    pump(5, 2, 3)
    pump(6, 1, 2)
    scatter_end(0, hidden, abuf.at[lo, x, core])
    gather_first(1, abuf)
    gather_second(1, abuf)
    pump(5, 3, depth)
    pump(6, 2, 3)
    pump(7, 1, 2)
    gather_third(1, abuf)
    pump(6, 3, depth)
    pump(7, 2, 3)
    gather_end(1, abuf)
    normalize(abuf, gain_b)
    for k in (0, 2, 1):
        finish(4 + k)
        in_project(wb, k)
    in_product()

    def same_group(shape):
        return lax.div(iota(shape, 0), modes) == lax.div(iota(shape, 1), per)

    side = tile_groups * modes
    mine = pair * 2 + y
    for b in range(2):
        for q in range(tiles):
            at = slice(q * LANES, (q + 1) * LANES)
            values = xin[b * tokens : (b + 1) * tokens, at].astype(f32)
            ends = dot(to_end[q * side : (q + 1) * side, :], values, highest)
            ends = jnp.where(same_group((side, LANES)), ends, 0.0)
            total = ends[0:modes]
            for g in range(1, tile_groups):
                total = total + ends[g * modes : (g + 1) * modes]
            states[mine, b, :, at] = total

    def state_copy(off, index, to):
        return remote(
            states.at[index],
            states.at[index],
            state_send.at[off - 1],
            state_recv.at[off - 1],
            {"ctx": (lax.div(to, 2) * 2 + lo) * 2 + lax.rem(to, 2)},
        )

    def state_start(off, carry):
        state_copy(off, mine, lax.rem(mine + off, depth)).start()
        return carry

    lax.fori_loop(1, depth, state_start, 0)
    pump(7, 3, depth)

    def long_tile(q, carry):
        at = lanes(q)
        values = jnp.concatenate([xin[0:tokens, at], xin[tokens : 2 * tokens, at]], axis=1)
        group_of = lax.div(lax.rem(iota((tokens, 2 * LANES), 1), LANES), per)
        total = jnp.zeros((tokens, 2 * LANES), f32)
        for g in range(tile_groups):
            total = jnp.where(group_of == g, dot(toep_b[q * tile_groups + g], values), total)
        for b in range(2):
            conv[b * tokens : (b + 1) * tokens, at] = total[:, b * LANES : (b + 1) * LANES]
        return carry

    lax.fori_loop(0, tiles, long_tile, 0)

    def state_wait(off, carry):
        state_copy(off, lax.rem(mine - off + depth, depth), lax.rem(mine + off, depth)).wait_recv()
        return carry

    lax.fori_loop(1, depth, state_wait, 0)
    rates = rates_here[...]

    def state_add(index, totals):
        result = []
        for b in range(2):
            block = 4 * pair + 2 * b + y
            total = totals[b]
            for k in range(2):
                j = 4 * lax.div(index, 2) + 2 * k + lax.rem(index, 2)
                gap = jnp.maximum(block - 1 - j, 0).astype(f32) * tokens
                term = jnp.exp(-rates * gap) * states[index, k]
                total = total + jnp.where(j < block, term, jnp.zeros_like(term))
            result.append(total)
        return tuple(result)

    zero = jnp.zeros((modes, channels), f32)
    entering = lax.fori_loop(0, depth, state_add, (zero, zero))
    for b in range(2):
        for q in range(tiles):
            at = slice(q * LANES, (q + 1) * LANES)
            spread = jnp.concatenate([entering[b][:, at]] * tile_groups, axis=0)
            spread = jnp.where(same_group((side, LANES)), spread, 0.0)
            conv[b * tokens : (b + 1) * tokens, at] += dot(
                from_start[:, q * side : (q + 1) * side], spread, highest
            )
    product = proj[1] * conv[...]
    gated[...] = product.astype(bf16)
    finish(7)
    scatter_first(1, ob)
    give_back(1, product)
    scatter_second(1)
    scatter_third(1)
    scatter_end(1, abuf.at[lo, x, core], mixed)

    give_end(0)
    give_end(1)
    gated_a_out[...] = turned_out[0]
    gated_b_out[...] = turned_out[1]

    def state_sent(off, carry):
        state_copy(off, mine, lax.rem(mine + off, depth)).wait_send()
        return carry

    lax.fori_loop(1, depth, state_sent, 0)
    for stream in range(8):
        all_sent(stream)


def per_device(
    n,
    ntp,
    hidden,
    norm_gain_a,
    in_weight_a,
    mr_filter,
    out_weight_a,
    norm_gain_b,
    in_weight_b,
    li_rate,
    li_residue,
    out_weight_b,
):
    tokens, width = hidden.shape
    dn, channels = in_weight_a.shape[1:]
    on = out_weight_a.shape[1]
    features = width * ntp
    groups, taps = mr_filter.shape
    modes = li_rate.shape[1]
    half = channels // 2
    vmem = pl.BlockSpec(memory_space=pltpu.VMEM)
    anywhere = pl.BlockSpec(memory_space=pl.ANY)
    flops = 2 * tokens * features * channels * 8 + 2 * tokens * channels * (tokens + 2 * taps) * 8
    return pl.pallas_call(
        functools.partial(kernel, n, ntp),
        out_shape=(
            jax.ShapeDtypeStruct((tokens, width), bf16),
            jax.ShapeDtypeStruct((channels, tokens), bf16),
            jax.ShapeDtypeStruct((channels, tokens), bf16),
        ),
        in_specs=[vmem, vmem, anywhere, vmem, anywhere, vmem, anywhere, vmem, vmem, anywhere],
        out_specs=(vmem, vmem, vmem),
        scratch_shapes=[
            pltpu.VMEM((2, 3, features, half), bf16),
            pltpu.VMEM((2, n, half, on), bf16),
            pltpu.VMEM((2, 3, features, half), bf16),
            pltpu.VMEM((2, n, half, on), bf16),
            pltpu.VMEM((2, 2, 2, tokens, width), bf16),
            pltpu.VMEM((2, 2, 2, tokens, width), bf16),
            pltpu.VMEM((2 * tokens, features), bf16),
            pltpu.VMEM((3, 2 * tokens, half), f32),
            pltpu.VMEM((2 * tokens, half), bf16),
            pltpu.VMEM((3, taps, half), bf16),
            pltpu.VMEM((2 * tokens, half), f32),
            pltpu.VMEM((2 * tokens, half), bf16),
            pltpu.VMEM((2, 2, 2, tokens, width), bf16),
            pltpu.VMEM((2, 2, 2, tokens, width), bf16),
            pltpu.VMEM((2, 2, tokens, width), bf16),
            pltpu.VMEM((2, 2, 2, tokens // 2, width), bf16),
            pltpu.VMEM((2, 2, tokens // 2, width), bf16),
            pltpu.VMEM((2, 2, tokens // 2, width), bf16),
            pltpu.VMEM((2, half, tokens), bf16),
            pltpu.VMEM((2, channels, tokens), bf16),
            pltpu.VMEM((n // 2, 2, modes, half), f32),
            pltpu.VMEM((groups // 2, taps, 2 * taps), bf16),
            pltpu.VMEM((groups // 2, tokens, tokens), bf16),
            pltpu.VMEM((groups, taps), f32),
            pltpu.VMEM((groups, tokens), f32),
            pltpu.VMEM((groups // 2 * modes, tokens), f32),
            pltpu.VMEM((tokens, groups // 2 * modes), f32),
            pltpu.VMEM((modes, half), f32),
            pltpu.SemaphoreType.DMA((8, 2, 2, n // 2)),
            pltpu.SemaphoreType.DMA((8, 2, 2, n // 2)),
            pltpu.SemaphoreType.DMA((8, 2, n // 2)),
            pltpu.SemaphoreType.DMA((8, 2, n // 2)),
            pltpu.SemaphoreType.DMA((5, 5)),
            pltpu.SemaphoreType.DMA((5, 5)),
            pltpu.SemaphoreType.DMA((n // 2 - 1,)),
            pltpu.SemaphoreType.DMA((n // 2 - 1,)),
            pltpu.SemaphoreType.DMA((3,)),
            pltpu.SemaphoreType.DMA((3,)),
            pltpu.SemaphoreType.DMA((8,)),
        ],
        cost_estimate=pl.CostEstimate(flops=flops, bytes_accessed=32 * 1024 * 1024, transcendentals=0),
        compiler_params=pltpu.CompilerParams(
            collective_id=0, has_side_effects=True, vmem_limit_bytes=60 * 1024 * 1024
        ),
    )(
        hidden,
        norm_gain_a.reshape(1, -1),
        in_weight_a,
        mr_filter,
        out_weight_a,
        norm_gain_b.reshape(1, -1),
        in_weight_b,
        li_rate,
        li_residue,
        out_weight_b,
    )


def solution(mesh):
    in_specs = (
        P("ctx", "tp"),
        P(),
        P(None, "ctx", "tp"),
        P("tp", None),
        P("tp", "ctx"),
        P(),
        P(None, "ctx", "tp"),
        P("tp", None),
        P("tp", None),
        P("tp", "ctx"),
    )
    out_specs = (P("ctx", "tp"), P("tp", "ctx"), P("tp", "ctx"))
    return jax.shard_map(
        functools.partial(per_device, mesh.shape["ctx"], mesh.shape["tp"]),
        mesh=mesh,
        in_specs=in_specs,
        out_specs=out_specs,
        check_vma=False,
    )
```

```python
import functools

import jax
import jax.numpy as jnp
from jax import lax
from jax.experimental import pallas as pl
from jax.experimental.pallas import tpu as pltpu
from jax.sharding import PartitionSpec as P

LANES = 128
MESH = pl.DeviceIdType.MESH
f32 = jnp.float32
bf16 = jnp.bfloat16
highest = lax.Precision.HIGHEST


def dot(a, b, precision=None):
    return lax.dot_general(
        a, b, (((1,), (0,)), ((), ())), precision=precision, preferred_element_type=f32
    )


def iota(shape, dim):
    return lax.broadcasted_iota(jnp.int32, shape, dim)


def kernel(
    n,
    ntp,
    hidden,
    gain_a,
    win_a,
    mr_filter,
    wout_a,
    gain_b,
    win_b,
    rate_in,
    residue_in,
    wout_b,
    mixed,
    gated_a_out,
    gated_b_out,
    wa,
    oa,
    wb,
    ob,
    hbuf,
    abuf,
    normed,
    proj,
    xin,
    halos,
    conv,
    gated,
    part,
    from_core,
    core_sum,
    from_first,
    first_sum,
    from_last,
    turned,
    turned_out,
    states,
    toep_a,
    toep_b,
    rows_a,
    rows_b,
    to_end,
    from_start,
    rates_here,
    rate,
    residue,
    line_send,
    line_recv,
    cross_send,
    cross_recv,
    swap_send,
    swap_recv,
    state_send,
    state_recv,
    halo_send,
    halo_recv,
    local_sems,
):
    me = lax.axis_index("ctx")
    mytp = lax.axis_index("tp")
    tokens, width = hidden.shape
    all_channels = win_a.shape[2]
    channels = all_channels // 2
    dn = win_a.shape[1]
    on = wout_a.shape[1]
    features = width * ntp
    all_groups, taps = mr_filter.shape
    groups = all_groups // 2
    modes = rate_in.shape[1]
    per = channels // groups
    tile_groups = LANES // per
    tiles = channels // LANES
    blocks = tokens // taps
    depth = n // 2
    rows2 = tokens // 2

    z, y = lax.div(me, 2), lax.rem(me, 2)
    lo = lax.rem(z, 2)
    pair = lax.div(z, 2)
    x, core = lax.div(mytp, 2), lax.rem(mytp, 2)
    core_peer = {"tp": x * 2 + 1 - core}
    x_peer = {"tp": (1 - x) * 2 + core}
    z_peer = {"ctx": (z + 1 - 2 * lo) * 2 + y}
    y_peer = {"ctx": z * 2 + 1 - y}

    barrier = pltpu.get_barrier_semaphore()

    def greet_ctx(off, carry):
        pl.semaphore_signal(
            barrier, inc=1, device_id={"ctx": lax.rem(me + off, n)}, device_id_type=MESH
        )
        return carry

    lax.fori_loop(1, n, greet_ctx, 0)
    for peer in (core_peer, x_peer):
        pl.semaphore_signal(barrier, inc=1, device_id=peer, device_id_type=MESH)

    def remote(src, dst, send, recv, peer):
        return pltpu.make_async_remote_copy(
            src_ref=src,
            dst_ref=dst,
            send_sem=send,
            recv_sem=recv,
            device_id=peer,
            device_id_type=MESH,
        )

    def buffers(stream):
        return ((win_a, wa, wout_a, oa), (win_b, wb, wout_b, ob))[stream // 4]

    def slot(stream, h, owner):
        if stream % 4 < 3:
            rows = pl.ds(pl.multiple_of(owner * dn, dn), dn)
            return buffers(stream)[1].at[h, stream % 4, rows, :]
        return buffers(stream)[3].at[h, owner]

    def own(stream, h):
        at = pl.ds(pl.multiple_of(h * channels, channels), channels)
        if stream % 4 < 3:
            return buffers(stream)[0].at[stream % 4, :, at]
        return buffers(stream)[2].at[at, :]

    def along(way):
        return (z, 1) if way == 0 else (depth - 1 - z, -1)

    def line_copy(stream, way, kind, step, first=False):
        zz, d = along(way)
        h = 1 - lo if kind == 0 else lo
        owner = (z - d * step) * 2 + y
        return remote(
            own(stream, h) if first else slot(stream, h, owner),
            slot(stream, h, owner),
            line_send.at[stream, way, kind, step],
            line_recv.at[stream, way, kind, step],
            {"ctx": (z + d) * 2 + y},
        )

    def line_arrival(stream, way, kind, step):
        zz, d = along(way)
        h = lo if kind == 0 else 1 - lo
        here = slot(stream, h, (z - d * (step + 1)) * 2 + y)
        return remote(
            here,
            here,
            line_send.at[stream, way, kind, step],
            line_recv.at[stream, way, kind, step],
            {"ctx": (z - d) * 2 + y},
        )

    def cross_copy(stream, way, step, side):
        zz, d = along(way)
        here = slot(stream, lo, (z - d * step) * 2 + side)
        return remote(
            here, here, cross_send.at[stream, way, step], cross_recv.at[stream, way, step], y_peer
        )

    def cross_own(stream):
        return remote(
            own(stream, lo),
            slot(stream, lo, me),
            cross_send.at[stream, 0, 0],
            cross_recv.at[stream, 0, 0],
            y_peer,
        )

    def start(stream):
        for kind in (1, 0):
            for way in (0, 1):
                zz, d = along(way)

                @pl.when(zz + 1 + kind < depth)
                def ahead():
                    line_copy(stream, way, kind, 0, True).start()

        cross_own(stream).start()

    def pump(stream, low, high):
        def body(step, carry):
            for way in (0, 1):
                zz, d = along(way)

                @pl.when(zz - step >= 0)
                def arrived():
                    line_arrival(stream, way, 0, step - 1).wait_recv()

                    @pl.when(zz + 2 < depth)
                    def through():
                        line_copy(stream, way, 1, step).start()

                    cross_copy(stream, way, step, y).start()

                    @pl.when(zz + 1 < depth)
                    def near():
                        line_arrival(stream, way, 1, step - 1).wait_recv()
                        line_copy(stream, way, 0, step).start()

            return carry

        if min(high, depth) > low:
            lax.fori_loop(low, min(high, depth), body, 0)

    def finish(stream):
        cross_copy(stream, 0, 0, 1 - y).wait_recv()

        def body(step, carry):
            for way in (0, 1):
                zz, d = along(way)

                @pl.when(zz - step >= 0)
                def arrived():
                    cross_copy(stream, way, step, 1 - y).wait_recv()

            return carry

        lax.fori_loop(1, depth, body, 0)
        own_copy(stream).wait()

    def all_sent(stream):
        cross_own(stream).wait_send()

        def body(step, carry):
            for way in (0, 1):
                zz, d = along(way)

                @pl.when(zz - step >= 0)
                def passed():
                    @pl.when(zz + 1 < depth)
                    def near():
                        line_copy(stream, way, 0, step).wait_send()

                    @pl.when(zz + 2 < depth)
                    def through():
                        line_copy(stream, way, 1, step).wait_send()

                    @pl.when(step > 0)
                    def crossed():
                        cross_copy(stream, way, step, y).wait_send()

            return carry

        lax.fori_loop(0, depth, body, 0)

    def own_copy(stream):
        return pltpu.make_async_copy(own(stream, lo), slot(stream, lo, me), local_sems.at[stream])

    upper, lower = pl.ds(0, rows2), pl.ds(rows2, rows2)

    def swap(use, step, src, dst, peer):
        return remote(src, dst, swap_send.at[use, step], swap_recv.at[use, step], peer)

    def gather_moves(use, buffer):
        def move(step, ref_out, ref_in, peer):
            return (swap(use, step, ref_out, ref_out, peer), swap(use, step, ref_in, ref_in, peer))

        return (
            move(0, buffer.at[lo, x, core, upper], buffer.at[1 - lo, x, core, upper], z_peer),
            move(1, buffer.at[lo, x, core, lower], buffer.at[lo, 1 - x, core, lower], x_peer),
            move(2, buffer.at[:, x, core, upper], buffer.at[:, 1 - x, core, upper], x_peer),
            move(3, buffer.at[lo, :, core, lower], buffer.at[1 - lo, :, core, lower], z_peer),
            move(4, buffer.at[:, :, core], buffer.at[:, :, 1 - core], core_peer),
        )

    def gather_first(use, buffer):
        moves = gather_moves(use, buffer)
        moves[0][0].start()
        moves[1][0].start()

    def gather_second(use, buffer):
        moves = gather_moves(use, buffer)
        moves[0][1].wait_recv()
        moves[2][0].start()
        moves[1][1].wait_recv()
        moves[3][0].start()

    def gather_third(use, buffer):
        moves = gather_moves(use, buffer)
        moves[2][1].wait_recv()
        moves[3][1].wait_recv()
        moves[4][0].start()

    def gather_end(use, buffer):
        moves = gather_moves(use, buffer)
        moves[4][1].wait_recv()
        for out, into in moves:
            out.wait_send()

    def normalize(buffer, gain):
        for b in range(2):
            total = jnp.zeros((tokens, 1), f32)
            for block in range(ntp):
                wide = buffer[b, block // 2, block % 2].astype(f32)
                total = total + jnp.sum(wide * wide, axis=1, keepdims=True)
            factor = lax.rsqrt(total / features + 1e-06)
            for block in range(ntp):
                at = slice(block * width, (block + 1) * width)
                wide = buffer[b, block // 2, block % 2].astype(f32)
                normed[b * tokens : (b + 1) * tokens, at] = (wide * factor * gain[:, at]).astype(bf16)

    def in_project(weight, k):
        proj[k] = dot(normed[...], weight[lo, k])

    def in_product():
        xin[...] = (proj[0] * proj[2]).astype(bf16)

    def out_blocks(buffer, c):
        def body(xx, carry):
            for j in range(width // on):
                block = dot(gated[...], buffer[lo, (xx * 2 + c) * (width // on) + j]).astype(bf16)
                for b in range(2):
                    part[b, xx, c, :, j * on : (j + 1) * on] = block[b * tokens : (b + 1) * tokens]
            return carry

        lax.fori_loop(0, 2, body, 0)

    def scatter_moves(which):
        use = 2 + which
        return (
            swap(use, 0, part.at[:, :, 1 - core], from_core.at[which], core_peer),
            swap(use, 1, core_sum.at[1 - lo, :, upper], from_first.at[which, 0], z_peer),
            swap(use, 2, core_sum.at[:, 1 - x, lower], from_first.at[which, 1], x_peer),
            swap(use, 3, first_sum.at[0, 1 - x], from_last.at[which, 0], x_peer),
            swap(use, 4, first_sum.at[1, 1 - lo], from_last.at[which, 1], z_peer),
        )

    def scatter_first(which, buffer):
        moves = scatter_moves(which)
        out_blocks(buffer, 1 - core)
        moves[0].start()
        out_blocks(buffer, core)

    def scatter_second(which):
        moves = scatter_moves(which)
        moves[0].wait_recv()

        def add(b, xx, at):
            core_sum[b, xx, at] = (
                part[b, xx, core, at].astype(f32) + from_core[which, b, xx, at].astype(f32)
            ).astype(bf16)

        for xx in range(2):
            add(1 - lo, xx, upper)
        moves[1].start()
        for b in range(2):
            add(b, 1 - x, lower)
        moves[2].start()
        for xx in range(2):
            add(lo, xx, upper)
        for b in range(2):
            add(b, x, lower)

    def scatter_third(which):
        moves = scatter_moves(which)
        moves[1].wait_recv()
        for xx in range(2):
            first_sum[0, xx] = (
                core_sum[lo, xx, upper].astype(f32) + from_first[which, 0, xx].astype(f32)
            ).astype(bf16)
        moves[3].start()
        moves[2].wait_recv()
        for b in range(2):
            first_sum[1, b] = (
                core_sum[b, x, lower].astype(f32) + from_first[which, 1, b].astype(f32)
            ).astype(bf16)
        moves[4].start()

    def scatter_end(which, base, out):
        moves = scatter_moves(which)
        moves[3].wait_recv()
        out[upper] = (
            base[upper].astype(f32) + first_sum[0, x].astype(f32) + from_last[which, 0].astype(f32)
        ).astype(bf16)
        moves[4].wait_recv()
        out[lower] = (
            base[lower].astype(f32) + first_sum[1, lo].astype(f32) + from_last[which, 1].astype(f32)
        ).astype(bf16)
        for move in moves:
            move.wait_send()

    def give_move(which):
        return swap(
            4, which, turned.at[which], turned_out.at[which, pl.ds(pl.multiple_of(lo * channels, channels), channels)], z_peer
        )

    def give_back(which, product):
        flat = product.T.astype(bf16)
        at = pl.ds(pl.multiple_of(lo * channels, channels), channels)
        own_block = jnp.where(lo == 0, flat[:, :tokens], flat[:, tokens:])
        other = jnp.where(lo == 0, flat[:, tokens:], flat[:, :tokens])
        turned[which] = other
        turned_out[which, at] = own_block
        give_move(which).start()

    def give_end(which):
        give_move(which).wait_send()
        arriving = turned_out.at[which, pl.ds(pl.multiple_of((1 - lo) * channels, channels), channels)]
        swap(4, which, turned.at[which], arriving, z_peer).wait_recv()

    def lanes(q):
        return pl.ds(pl.multiple_of(q * LANES, LANES), LANES)

    filter_copies = (
        pltpu.make_async_copy(rate_in, rate, local_sems.at[8]),
        pltpu.make_async_copy(residue_in, residue, local_sems.at[9]),
    )
    for copy in filter_copies:
        copy.start()
    hbuf[lo, x, core] = hidden[...]
    for stream in range(8):
        own_copy(stream).start()
    pl.semaphore_wait(barrier, (n - 1) + 2)

    gather_first(0, hbuf)
    start(0)
    start(1)

    flip = (lax.rem(iota((taps, taps), 0) + iota((taps, taps), 1), taps) == 0).astype(bf16)
    rows_a[...] = dot(mr_filter[...], flip)
    for copy in filter_copies:
        copy.wait()
    lag = lax.rem(tokens - iota((all_groups, tokens), 1), tokens).astype(f32)
    impulse = jnp.zeros((all_groups, tokens), f32)
    for m in range(modes):
        r = rate[:, m : m + 1]
        impulse = impulse + residue[:, m : m + 1] * jnp.sqrt(2.0 * r) * jnp.exp(-r * lag)
    rows_b[...] = impulse

    def build_a(g, carry):
        row = jnp.broadcast_to(rows_a[pl.ds(lo * groups + g, 1), :], (taps, taps))
        rolled = pltpu.roll(row, 0, 1, stride=1, stride_axis=0)
        below = iota((taps, taps), 1) <= iota((taps, taps), 0)
        toep_a[g, :, :taps] = jnp.where(below, 0.0, rolled).astype(bf16)
        toep_a[g, :, taps:] = jnp.where(below, rolled, 0.0).astype(bf16)
        return carry

    def build_b(g, carry):
        row = jnp.broadcast_to(rows_b[pl.ds(lo * groups + g, 1), :], (tokens, tokens))
        rolled = pltpu.roll(row, 0, 1, stride=1, stride_axis=0)
        below = iota((tokens, tokens), 1) <= iota((tokens, tokens), 0)
        toep_b[g] = jnp.where(below, rolled, 0.0).astype(bf16)
        return carry

    lax.fori_loop(0, groups, build_a, 0)
    pump(0, 1, 2)
    start(2)
    gather_second(0, hbuf)
    lax.fori_loop(0, groups, build_b, 0)
    pump(0, 2, 3)
    pump(1, 1, 2)
    gather_third(0, hbuf)

    def mode_row(ref):
        here = ref[pl.ds(pl.multiple_of(lo * groups, 8), groups), :]
        shape = (modes, groups * modes)
        pick = (iota(shape, 0) == lax.rem(iota(shape, 1), modes)).astype(f32)
        spread = dot(here, pick, highest)
        keep = iota(spread.shape, 0) == lax.div(iota(spread.shape, 1), modes)
        return jnp.sum(jnp.where(keep, spread, 0.0), axis=0, keepdims=True)

    rate_row = mode_row(rate)
    weight_row = mode_row(residue) * jnp.sqrt(2.0 * rate_row)
    shape = (modes, groups * modes)
    by_mode = jnp.where(iota(shape, 0) == lax.rem(iota(shape, 1), modes), rate_row, 0.0)
    shape = (groups * modes, channels)
    pick = (lax.div(iota(shape, 0), modes) == lax.div(iota(shape, 1), per)).astype(f32)
    rates_here[...] = dot(by_mode, pick, highest)
    position = iota((tokens, groups * modes), 0).astype(f32)
    from_start[...] = weight_row * jnp.exp(-rate_row * (position + 1.0))
    to_end[...] = jnp.exp(-rate_row * (tokens - 1.0 - position)).T

    pump(0, 3, depth)
    pump(1, 2, 3)
    pump(2, 1, 2)
    start(3)
    gather_end(0, hbuf)
    normalize(hbuf, gain_a)
    pump(1, 3, depth)
    pump(2, 2, 3)
    start(4)
    finish(0)
    in_project(wa, 0)
    pump(3, 1, 2)
    start(5)
    finish(1)
    in_project(wa, 1)
    pump(2, 3, depth)
    finish(2)
    in_project(wa, 2)
    in_product()

    def tail(b):
        return xin.at[pl.ds((b + 1) * tokens - taps, taps), :]

    halo_moves = (
        remote(tail(0), halos.at[0], halo_send.at[0], halo_recv.at[0], y_peer),
        remote(tail(1), halos.at[1], halo_send.at[1], halo_recv.at[1], y_peer),
        remote(
            tail(1),
            halos.at[2],
            halo_send.at[2],
            halo_recv.at[2],
            {"ctx": lax.rem(z + 2, depth) * 2 + 1 - y},
        ),
    )
    for move in halo_moves:
        move.start()
    pump(3, 2, 3)
    pump(4, 1, 2)
    start(6)
    pump(3, 3, depth)
    pump(4, 2, 3)
    pump(5, 1, 2)
    start(7)
    for move in halo_moves:
        move.wait()

    def medium_tile(q, carry):
        at = lanes(q)
        near0, near1, far = halos[0, :, at], halos[1, :, at], halos[2, :, at]
        far = jnp.where(z >= 2, far, jnp.zeros_like(far))
        befores = (jnp.where(y == 1, near0, far), jnp.where(y == 1, near1, near0))
        here, early = [], []
        for b in range(2):
            mine = [
                xin[b * tokens + k * taps : b * tokens + (k + 1) * taps, at] for k in range(blocks)
            ]
            here = here + mine
            early = early + [befores[b]] + mine[:-1]
        window = jnp.concatenate(
            [jnp.concatenate(early, axis=1), jnp.concatenate(here, axis=1)], axis=0
        )
        shape = (taps, 2 * blocks * LANES)
        group_of = lax.div(lax.rem(iota(shape, 1), LANES), per)
        total = jnp.zeros(shape, f32)
        for g in range(tile_groups):
            total = jnp.where(group_of == g, dot(toep_a[q * tile_groups + g], window), total)
        for k in range(2 * blocks):
            conv[k * taps : (k + 1) * taps, at] = total[:, k * LANES : (k + 1) * LANES]
        return carry

    lax.fori_loop(0, tiles, medium_tile, 0)
    product = proj[1] * conv[...]
    gated[...] = product.astype(bf16)
    finish(3)
    scatter_first(0, oa)
    give_back(0, product)
    scatter_second(0)
    scatter_third(0)
    pump(4, 3, depth)
    pump(5, 2, 3)
    pump(6, 1, 2)
    scatter_end(0, hidden, abuf.at[lo, x, core])
    gather_first(1, abuf)
    gather_second(1, abuf)
    pump(5, 3, depth)
    pump(6, 2, 3)
    pump(7, 1, 2)
    gather_third(1, abuf)
    pump(6, 3, depth)
    pump(7, 2, 3)
    gather_end(1, abuf)
    normalize(abuf, gain_b)
    for k in (0, 2, 1):
        finish(4 + k)
        in_project(wb, k)
    in_product()

    def same_group(shape):
        return lax.div(iota(shape, 0), modes) == lax.div(iota(shape, 1), per)

    side = tile_groups * modes
    mine = pair * 2 + y
    for b in range(2):
        for q in range(tiles):
            at = slice(q * LANES, (q + 1) * LANES)
            values = xin[b * tokens : (b + 1) * tokens, at].astype(f32)
            ends = dot(to_end[q * side : (q + 1) * side, :], values, highest)
            ends = jnp.where(same_group((side, LANES)), ends, 0.0)
            total = ends[0:modes]
            for g in range(1, tile_groups):
                total = total + ends[g * modes : (g + 1) * modes]
            states[mine, b, :, at] = total

    def state_copy(off, index, to):
        return remote(
            states.at[index],
            states.at[index],
            state_send.at[off - 1],
            state_recv.at[off - 1],
            {"ctx": (lax.div(to, 2) * 2 + lo) * 2 + lax.rem(to, 2)},
        )

    def state_start(off, carry):
        state_copy(off, mine, lax.rem(mine + off, depth)).start()
        return carry

    lax.fori_loop(1, depth, state_start, 0)
    pump(7, 3, depth)

    def long_tile(q, carry):
        at = lanes(q)
        values = jnp.concatenate([xin[0:tokens, at], xin[tokens : 2 * tokens, at]], axis=1)
        group_of = lax.div(lax.rem(iota((tokens, 2 * LANES), 1), LANES), per)
        total = jnp.zeros((tokens, 2 * LANES), f32)
        for g in range(tile_groups):
            total = jnp.where(group_of == g, dot(toep_b[q * tile_groups + g], values), total)
        for b in range(2):
            conv[b * tokens : (b + 1) * tokens, at] = total[:, b * LANES : (b + 1) * LANES]
        return carry

    lax.fori_loop(0, tiles, long_tile, 0)

    def state_wait(off, carry):
        state_copy(off, lax.rem(mine - off + depth, depth), lax.rem(mine + off, depth)).wait_recv()
        return carry

    lax.fori_loop(1, depth, state_wait, 0)
    rates = rates_here[...]

    def state_add(index, totals):
        result = []
        for b in range(2):
            block = 4 * pair + 2 * b + y
            total = totals[b]
            for k in range(2):
                j = 4 * lax.div(index, 2) + 2 * k + lax.rem(index, 2)
                gap = jnp.maximum(block - 1 - j, 0).astype(f32) * tokens
                term = jnp.exp(-rates * gap) * states[index, k]
                total = total + jnp.where(j < block, term, jnp.zeros_like(term))
            result.append(total)
        return tuple(result)

    zero = jnp.zeros((modes, channels), f32)
    entering = lax.fori_loop(0, depth, state_add, (zero, zero))
    for b in range(2):
        for q in range(tiles):
            at = slice(q * LANES, (q + 1) * LANES)
            spread = jnp.concatenate([entering[b][:, at]] * tile_groups, axis=0)
            spread = jnp.where(same_group((side, LANES)), spread, 0.0)
            conv[b * tokens : (b + 1) * tokens, at] += dot(
                from_start[:, q * side : (q + 1) * side], spread, highest
            )
    product = proj[1] * conv[...]
    gated[...] = product.astype(bf16)
    finish(7)
    scatter_first(1, ob)
    give_back(1, product)
    scatter_second(1)
    scatter_third(1)
    scatter_end(1, abuf.at[lo, x, core], mixed)

    give_end(0)
    give_end(1)
    gated_a_out[...] = turned_out[0]
    gated_b_out[...] = turned_out[1]

    def state_sent(off, carry):
        state_copy(off, mine, lax.rem(mine + off, depth)).wait_send()
        return carry

    lax.fori_loop(1, depth, state_sent, 0)
    for stream in range(8):
        all_sent(stream)


def per_device(
    n,
    ntp,
    hidden,
    norm_gain_a,
    in_weight_a,
    mr_filter,
    out_weight_a,
    norm_gain_b,
    in_weight_b,
    li_rate,
    li_residue,
    out_weight_b,
):
    tokens, width = hidden.shape
    dn, channels = in_weight_a.shape[1:]
    on = out_weight_a.shape[1]
    features = width * ntp
    groups, taps = mr_filter.shape
    modes = li_rate.shape[1]
    half = channels // 2
    vmem = pl.BlockSpec(memory_space=pltpu.VMEM)
    anywhere = pl.BlockSpec(memory_space=pl.ANY)
    flops = 2 * tokens * features * channels * 8 + 2 * tokens * channels * (tokens + 2 * taps) * 8
    return pl.pallas_call(
        functools.partial(kernel, n, ntp),
        out_shape=(
            jax.ShapeDtypeStruct((tokens, width), bf16),
            jax.ShapeDtypeStruct((channels, tokens), bf16),
            jax.ShapeDtypeStruct((channels, tokens), bf16),
        ),
        in_specs=[vmem, vmem, anywhere, vmem, anywhere, vmem, anywhere, anywhere, anywhere, anywhere],
        out_specs=(vmem, vmem, vmem),
        scratch_shapes=[
            pltpu.VMEM((2, 3, features, half), bf16),
            pltpu.VMEM((2, n, half, on), bf16),
            pltpu.VMEM((2, 3, features, half), bf16),
            pltpu.VMEM((2, n, half, on), bf16),
            pltpu.VMEM((2, 2, 2, tokens, width), bf16),
            pltpu.VMEM((2, 2, 2, tokens, width), bf16),
            pltpu.VMEM((2 * tokens, features), bf16),
            pltpu.VMEM((3, 2 * tokens, half), f32),
            pltpu.VMEM((2 * tokens, half), bf16),
            pltpu.VMEM((3, taps, half), bf16),
            pltpu.VMEM((2 * tokens, half), f32),
            pltpu.VMEM((2 * tokens, half), bf16),
            pltpu.VMEM((2, 2, 2, tokens, width), bf16),
            pltpu.VMEM((2, 2, 2, tokens, width), bf16),
            pltpu.VMEM((2, 2, tokens, width), bf16),
            pltpu.VMEM((2, 2, 2, tokens // 2, width), bf16),
            pltpu.VMEM((2, 2, tokens // 2, width), bf16),
            pltpu.VMEM((2, 2, tokens // 2, width), bf16),
            pltpu.VMEM((2, half, tokens), bf16),
            pltpu.VMEM((2, channels, tokens), bf16),
            pltpu.VMEM((n // 2, 2, modes, half), f32),
            pltpu.VMEM((groups // 2, taps, 2 * taps), bf16),
            pltpu.VMEM((groups // 2, tokens, tokens), bf16),
            pltpu.VMEM((groups, taps), f32),
            pltpu.VMEM((groups, tokens), f32),
            pltpu.VMEM((groups // 2 * modes, tokens), f32),
            pltpu.VMEM((tokens, groups // 2 * modes), f32),
            pltpu.VMEM((modes, half), f32),
            pltpu.VMEM((groups, modes), f32),
            pltpu.VMEM((groups, modes), f32),
            pltpu.SemaphoreType.DMA((8, 2, 2, n // 2)),
            pltpu.SemaphoreType.DMA((8, 2, 2, n // 2)),
            pltpu.SemaphoreType.DMA((8, 2, n // 2)),
            pltpu.SemaphoreType.DMA((8, 2, n // 2)),
            pltpu.SemaphoreType.DMA((5, 5)),
            pltpu.SemaphoreType.DMA((5, 5)),
            pltpu.SemaphoreType.DMA((n // 2 - 1,)),
            pltpu.SemaphoreType.DMA((n // 2 - 1,)),
            pltpu.SemaphoreType.DMA((3,)),
            pltpu.SemaphoreType.DMA((3,)),
            pltpu.SemaphoreType.DMA((10,)),
        ],
        cost_estimate=pl.CostEstimate(flops=flops, bytes_accessed=32 * 1024 * 1024, transcendentals=0),
        compiler_params=pltpu.CompilerParams(
            collective_id=0, has_side_effects=True, vmem_limit_bytes=60 * 1024 * 1024
        ),
    )(
        hidden,
        norm_gain_a.reshape(1, -1),
        in_weight_a,
        mr_filter,
        out_weight_a,
        norm_gain_b.reshape(1, -1),
        in_weight_b,
        li_rate,
        li_residue,
        out_weight_b,
    )


def solution(mesh):
    in_specs = (
        P("ctx", "tp"),
        P(),
        P(None, "ctx", "tp"),
        P("tp", None),
        P("tp", "ctx"),
        P(),
        P(None, "ctx", "tp"),
        P("tp", None),
        P("tp", None),
        P("tp", "ctx"),
    )
    out_specs = (P("ctx", "tp"), P("tp", "ctx"), P("tp", "ctx"))
    return jax.shard_map(
        functools.partial(per_device, mesh.shape["ctx"], mesh.shape["tp"]),
        mesh=mesh,
        in_specs=in_specs,
        out_specs=out_specs,
        check_vma=False,
    )
```
